32 devices in a mesh: groups: 2 (over y), enc: 4 (over z), dec: 2 (over x), mp: 2 (over core).
Axes of the slice: x: 2, y: 2, z: 4, core: 2. Of those that a mesh axis runs over, the one named last changes fastest.
Arguments:
- tokens: bfloat16 [4, 16, 16, 16, 1280], P(('groups', 'dec'), 'enc'), parts along dimension 0, may hold values from -6 to 6
- gain_pre: float32 [1280], replicated, may hold values from 0.5 to 2
- w_up: bfloat16 [1280, 2560], P('enc', 'mp'), may hold values from -0.15625 to 0.15625
- w_down: bfloat16 [2560, 1280], P('mp', 'enc'), may hold values from -0.125 to 0.125
- gain_post: float32 [1280], replicated, may hold values from 0.5 to 2
- w_neck: bfloat16 [1280, 256], replicated, may hold values from -0.15625 to 0.15625
- conv_weight: bfloat16 [3, 3, 256, 256], P(None, None, None, 'mp'), may hold values from -0.125 to 0.125
- conv_bias: float32 [256], P('mp'), may hold values from -3 to 3
- cls_weight: bfloat16 [256, 13], P('mp'), may hold values from -0.375 to 0.375
- cls_bias: float32 [13], replicated, may hold values from -4 to 4
- tile_table: int32 [4, 16, 2], P(('groups', 'dec')), parts along dimension 0, may hold values from -1 to 16, as said below
- labels: int32 [8, 4, 96], P(None, 'enc', ('groups', 'dec')), parts along dimension 2, may hold values from 0 to 12
Outputs:
- logits: float32 [8, 4, 96, 13], P(None, 'enc', ('groups', 'dec')), parts along dimension 2
- nll: float32 [8, 4, 96], P(None, 'enc', ('groups', 'dec')), parts along dimension 2
The draws below stay inside these ranges and needn't reach their ends.
There are 2 independent parts, one for each index of `groups`. The reference program is written for one: setup_inputs(seed, part) draws one part's arguments, and reference() takes and returns one part's arrays. A program takes and returns all parts, laid end to end along the dimension named above; an argument that names none is the same for every part. Nothing has to cross between parts.
Inputs may be any that keep to these rules, and one draw needn't show every extreme that they name: `tile_table`: in every band each tile corner with strip row a multiple of 8 from 0 to 16 and band column 0 or 8 stands in exactly one slot; all other slots are empty; in every band one encoder rank holds 4 tiles.
All inputs are finite; a program needn't handle non-finite values.
Results may differ from the reference program's by a relative error of at most 0.0075.
Values may be sent and summed in bfloat16 or wider, within the bound.
A program may use at most 64 MiB of HBM per device.

```python
import math
import jax
import jax.numpy as jnp
from jax import lax

D = 1280
FF = 2560
C = 256
NCLS = 13
TS = 16
BAND = 24
TSLOT = 4
RS = 8
W_ALL = 48
N_ENC = 4
N_DEC = 2
N_MP = 2


def draw_tile_table(key, part):
    slots_all = N_ENC * TSLOT
    rows_strip = RS * N_ENC
    stride = TS // 2
    tile_total = 2 * ((rows_strip - TS) // stride + 1)
    band_keys = jax.random.split(jax.random.fold_in(key, 7), N_DEC)

    def one_band(band_key):
        key_order, key_heavy, key_spread = jax.random.split(band_key, 3)
        tile_order = jax.random.permutation(key_order, tile_total).astype(jnp.int32)
        heavy_rank = jax.random.randint(key_heavy, (), 0, N_ENC).astype(jnp.int32)
        spread = jax.random.permutation(key_spread, slots_all - TSLOT).astype(jnp.int32)
        others = spread[:tile_total - TSLOT]
        others = jnp.where(others < heavy_rank * TSLOT, others, others + TSLOT)
        slot_of = jnp.concatenate([heavy_rank * TSLOT + jnp.arange(TSLOT, dtype=jnp.int32), others])
        tile_rows = (stride * (tile_order // 2)).astype(jnp.int32)
        tile_cols = (stride * (tile_order % 2)).astype(jnp.int32)
        slot_table = jnp.full((slots_all, 2), -1, jnp.int32)
        slot_table = slot_table.at[slot_of, 0].set(tile_rows)
        slot_table = slot_table.at[slot_of, 1].set(tile_cols)
        return slot_table
    return jax.vmap(one_band)(band_keys)


def with_ends(entries, rng, low, largest):
    dims = entries.shape
    place = [jax.random.randint(jax.random.fold_in(rng, axis), (), 0, dims[axis]) for axis in range(len(dims))]
    entries = entries.at[tuple(place)].set(low)
    longest = dims.index(max(dims))
    place[longest] = (place[longest] + 1) % dims[longest]
    return entries.at[tuple(place)].set(largest)


def block_scale(stream_key, shape, cuts, low, largest):
    factor_of = 1.0
    for position, parts in cuts:
        draws = jax.random.uniform(jax.random.fold_in(jax.random.fold_in(stream_key, 6), position), (parts,), jnp.float32, low / len(cuts), largest / len(cuts))
        factor_of = factor_of * jnp.repeat(jnp.exp(draws), shape[position] // parts).reshape((-1,) + (1,) * (len(shape) - 1 - position))
    return factor_of


def scatter_about(own_key, dims, scale, reach, cuts=(), kind=jnp.bfloat16):
    values = scale * jax.random.normal(own_key, dims, jnp.float32)
    if cuts:
        values = values * block_scale(own_key, dims, cuts, -0.22, 0.18)
    return jnp.clip(values, -reach, reach).astype(kind)


def setup_inputs(seed: int = 0, part: int = 0) -> dict:
    key_list = jax.random.split(jax.random.key(seed), 13)
    part_keys = jax.random.split(jax.random.fold_in(key_list[12], part), 13)
    return {
        "tokens": scatter_about(part_keys[0], (N_DEC, N_ENC * TSLOT, TS, TS, D), 1.0, 6.0, ((0, 2), (1, 4))),
        "gain_pre": jnp.clip(jnp.exp(jax.random.uniform(key_list[1], (D,), jnp.float32, math.log(0.5), math.log(2.0))), 0.5, 2.0),
        "w_up": scatter_about(key_list[2], (D, FF), D ** -0.5, 0.15625, ((0, 4), (1, 2))),
        "w_down": scatter_about(key_list[3], (FF, D), FF ** -0.5, 0.125, ((0, 2), (1, 4))),
        "gain_post": jnp.clip(jnp.exp(jax.random.uniform(key_list[4], (D,), jnp.float32, math.log(0.5), math.log(2.0))), 0.5, 2.0),
        "w_neck": scatter_about(key_list[5], (D, C), D ** -0.5, 0.15625),
        "conv_weight": scatter_about(key_list[6], (3, 3, C, C), (9 * C) ** -0.5, 0.125, ((3, 2),)),
        "conv_bias": scatter_about(key_list[7], (C,), 0.5, 3.0, ((0, 2),), jnp.float32),
        "cls_weight": scatter_about(key_list[8], (C, NCLS), C ** -0.5, 0.375, ((0, 2),)),
        "cls_bias": scatter_about(key_list[9], (NCLS,), 1.0, 4.0, (), jnp.float32),
        "tile_table": draw_tile_table(jax.random.fold_in(jax.random.fold_in(key_list[12], part), 71), part),
        "labels": with_ends(jax.random.randint(part_keys[11], (RS, N_ENC, W_ALL), 0, NCLS), jax.random.fold_in(part_keys[11], 1), 0, NCLS - 1).astype(jnp.int32),
    }


norm_eps = 1e-05
blend_sigma = 4.0

def layer_norm(values, scale_vec):
    row_mean = lax.optimization_barrier(jnp.mean(values, axis=-1, keepdims=True))
    centered = values - row_mean
    row_var = lax.optimization_barrier(jnp.mean(centered * centered, axis=-1, keepdims=True))
    return centered * lax.rsqrt(row_var + norm_eps) * scale_vec

def blend_weight(row_pos, col_pos):
    middle = (TS - 1) / 2.0
    spread = ((row_pos - middle) ** 2 + (col_pos - middle) ** 2) / (2.0 * blend_sigma * blend_sigma)
    rounded = lax.optimization_barrier(jnp.exp(-spread).astype(jnp.bfloat16))
    return rounded.astype(jnp.float32)

def encode_band(band_tokens, band_table, gain_pre, w_up, w_down, gain_post, w_neck):
    rows_strip = RS * N_ENC
    stride = TS // 2
    tile_total = 2 * ((rows_strip - TS) // stride + 1)
    slot_ids = jnp.arange(N_ENC * TSLOT, dtype=jnp.int32)
    tile_ids = jnp.arange(tile_total, dtype=jnp.int32)
    matches = (band_table[None, :, 0] == stride * (tile_ids[:, None] // 2)) & (band_table[None, :, 1] == stride * (tile_ids[:, None] % 2))
    chosen = lax.optimization_barrier(jnp.sum(jnp.where(matches, slot_ids[None, :], 0), axis=1)).astype(jnp.int32)
    tile_tokens = jnp.take(band_tokens, chosen, axis=0)
    flat_tok = tile_tokens.reshape(-1, D).astype(jnp.float32)
    normed = layer_norm(flat_tok, gain_pre).astype(jnp.bfloat16)
    hidden = jax.nn.gelu(jnp.dot(normed, w_up, preferred_element_type=jnp.float32), approximate=False).astype(jnp.bfloat16)
    block_size = FF // N_MP
    branch = jnp.zeros(flat_tok.shape, jnp.float32)
    for member in range(N_MP):
        partial_value = jnp.dot(hidden[:, member * block_size:(member + 1) * block_size], w_down[member * block_size:(member + 1) * block_size], preferred_element_type=jnp.float32)
        branch = branch + lax.optimization_barrier(partial_value.astype(jnp.bfloat16)).astype(jnp.float32)
    features = layer_norm(flat_tok + branch, gain_post).astype(jnp.bfloat16)
    tile_maps = jnp.dot(features, w_neck, preferred_element_type=jnp.float32).astype(jnp.bfloat16).reshape(tile_total, TS, TS, C)
    grid_pos = jnp.arange(TS).astype(jnp.float32)
    weights = blend_weight(grid_pos[:, None], grid_pos[None, :])
    numer = jnp.zeros((rows_strip, BAND, C), jnp.float32)
    denom = jnp.zeros((rows_strip, BAND), jnp.float32)
    for tile_num in range(tile_total):
        row_top = stride * (tile_num // 2)
        col_left = stride * (tile_num % 2)
        numer = numer.at[row_top:row_top + TS, col_left:col_left + TS].add(tile_maps[tile_num].astype(jnp.float32) * weights[:, :, None])
        denom = denom.at[row_top:row_top + TS, col_left:col_left + TS].add(weights)
    return (numer / denom[:, :, None]).astype(jnp.bfloat16)

def reference(tokens, gain_pre, w_up, w_down, gain_post, w_neck, conv_weight, conv_bias, cls_weight, cls_bias, tile_table, labels):
    rows_strip = RS * N_ENC
    width_all = N_DEC * BAND

    def one_band(pair):
        return encode_band(pair[0], pair[1], gain_pre, w_up, w_down, gain_post, w_neck)
    banded = lax.map(one_band, (tokens, tile_table))
    merged = jnp.transpose(banded, (1, 0, 2, 3)).reshape(rows_strip, width_all, C)
    padded = jnp.pad(merged, ((1, 1), (1, 1), (0, 0)))
    conv_sum = jnp.zeros((rows_strip * width_all, C), jnp.float32)
    for row_off in range(3):
        for col_off in range(3):
            window = padded[row_off:row_off + rows_strip, col_off:col_off + width_all].reshape(-1, C)
            conv_sum = conv_sum + jnp.dot(window, conv_weight[row_off, col_off], preferred_element_type=jnp.float32)
    activ = jax.nn.relu(conv_sum + conv_bias).astype(jnp.bfloat16)
    logits = jnp.dot(activ, cls_weight, preferred_element_type=jnp.float32) + cls_bias
    logits = logits.reshape(RS, N_ENC, width_all, NCLS)
    classes = jnp.arange(NCLS, dtype=jnp.int32)
    picked = lax.optimization_barrier(jnp.sum(jnp.where(labels[..., None] == classes, logits, 0.0), axis=-1))
    nll = jnp.log(lax.optimization_barrier(jnp.sum(jnp.exp(logits), axis=-1))) - picked
    return (logits, nll)
```

```python
import functools

import jax
import jax.numpy as jnp
from jax import lax
from jax.experimental import pallas as pl
from jax.experimental.pallas import tpu as pltpu
from jax.sharding import PartitionSpec as P

TS = 16


norm_eps = 1e-05
blend_sigma = 4.0


def shifted(value, axis, by):
    length = lax.axis_size(axis)
    return lax.ppermute(value, axis, [(i, (i + by) % length) for i in range(length)])


def padded_2(value, sides, width):
    for axis, dim in sides:
        size, length = (lax.axis_size(axis), value.shape[dim])
        up = [(i, (i + 1) % size) for i in range(size - 1)]
        down = [(j, i) for i, j in up]
        last = lax.slice_in_dim(value, length - width, length, axis=dim)
        leading = lax.slice_in_dim(value, 0, width, axis=dim)
        before = lax.ppermute(last, axis, up)
        after = lax.ppermute(leading, axis, down)
        value = jnp.concatenate([before, value, after], axis=dim)
    return value


def layer_norm(values, scale_vec):
    row_mean = jnp.mean(values, axis=-1, keepdims=True)
    centered = values - row_mean
    row_var = jnp.mean(centered * centered, axis=-1, keepdims=True)
    return centered * lax.rsqrt(row_var + norm_eps) * scale_vec


def blend_weight(row_pos, col_pos):
    middle = (TS - 1) / 2.0
    spread = ((row_pos - middle) ** 2 + (col_pos - middle) ** 2) / (2.0 * blend_sigma * blend_sigma)
    rounded = lax.optimization_barrier(jnp.exp(-spread).astype(jnp.bfloat16))
    return rounded.astype(jnp.float32)


MESH = pl.DeviceIdType.MESH
COLS = 256


def mlp_kernel(
    sizes, tok, gain_pre, w_up, w_down_t, gain_post, w_neck, out,
    weights, xs, normed, hidden, give, take, own, neck,
    local_sem, recv_sem, send_sem, give_sem, take_sem,
):
    groups, enc, dec = sizes
    y, z = lax.axis_index("groups"), lax.axis_index("enc")
    x, m = lax.axis_index("dec"), lax.axis_index("mp")
    blk, ff = w_up.shape
    total, width = xs.shape
    half = total // 2
    split = groups % 2 == 0 and dec % 2 == 0 and blk % 64 == 0
    parts = 4 if split else 1
    piece = blk // parts
    ox, oy = x + 1 - 2 * (x % 2), y + 1 - 2 * (y % 2)
    mine = (y % 2) * 2 + x % 2 if split else 0
    of_x = (y % 2) * 2 + 1 - x % 2
    of_y = (1 - y % 2) * 2 + x % 2
    diagonal = (1 - y % 2) * 2 + 1 - x % 2

    def region(mat, block, quarter):
        start = pl.multiple_of(block * blk + quarter * piece, 16)
        return weights.at[mat, pl.ds(start, piece)]

    def copy(mat, block, quarter, kind, target, sent, own_src=False):
        dst = region(mat, block, quarter)
        src = dst
        if own_src:
            start = pl.multiple_of(quarter * piece, 16)
            src = (w_up, w_down_t)[mat].at[pl.ds(start, piece)]
        return pltpu.make_async_remote_copy(
            src_ref=src, dst_ref=dst,
            send_sem=send_sem.at[mat, block, sent], recv_sem=recv_sem.at[mat, block, kind],
            device_id=target, device_id_type=MESH,
        )

    up_z, down_z = {"enc": z + 1}, {"enc": z - 1}
    to_x, to_y = {"dec": ox}, {"groups": oy}

    def own_sends(mat):
        right = copy(mat, z, mine, 0, up_z, 0, True)
        left = copy(mat, z, mine, 0, down_z, 1, True)
        return right, left

    def start_own(mat):
        right, left = own_sends(mat)

        @pl.when(z < enc - 1)
        def _():
            right.start()

        @pl.when(z > 0)
        def _():
            left.start()

    def z_step(mat, far):
        @pl.when(z - far >= 0)
        def _():
            block = z - far
            copy(mat, block, mine, 0, up_z, 0).wait_recv()

            @pl.when(z < enc - 1)
            def _():
                copy(mat, block, mine, 0, up_z, 0).start()

            if split:
                copy(mat, block, mine, 1, to_x, 2).start()
                copy(mat, block, mine, 2, to_y, 3).start()

        @pl.when(z + far < enc)
        def _():
            block = z + far
            copy(mat, block, mine, 0, down_z, 1).wait_recv()

            @pl.when(z > 0)
            def _():
                copy(mat, block, mine, 0, down_z, 1).start()

            if split:
                copy(mat, block, mine, 1, to_x, 2).start()
                copy(mat, block, mine, 2, to_y, 3).start()

    def each_block(far, fn):
        @pl.when(z - far >= 0)
        def _():
            fn(z - far)

        @pl.when(z + far < enc)
        def _():
            fn(z + far)

    def plane_step(mat, far):
        if not split:
            return

        def one(block):
            by_y = (block + mat) % 2 == 0
            copy(mat, block, of_x, 1, to_x, 2).wait_recv()

            @pl.when(by_y)
            def _():
                copy(mat, block, of_x, 3, to_y, 4).start()

            copy(mat, block, of_y, 2, to_y, 3).wait_recv()

            @pl.when(jnp.logical_not(by_y))
            def _():
                copy(mat, block, of_y, 3, to_x, 4).start()

        each_block(far, one)

    def diagonal_step(mat, far):
        if split:
            each_block(far, lambda block: copy(mat, block, diagonal, 3, to_x, 4).wait_recv())

    def finish_sends(mat):
        right, left = own_sends(mat)

        @pl.when(z < enc - 1)
        def _():
            right.wait_send()

        @pl.when(z > 0)
        def _():
            left.wait_send()

        for far in range(1, enc):
            @pl.when((z - far >= 0) & (z < enc - 1))
            def _(far=far):
                copy(mat, z - far, mine, 0, up_z, 0).wait_send()

            @pl.when((z + far < enc) & (z > 0))
            def _(far=far):
                copy(mat, z + far, mine, 0, down_z, 1).wait_send()

            if split:
                def one(block):
                    copy(mat, block, mine, 1, to_x, 2).wait_send()
                    copy(mat, block, mine, 2, to_y, 3).wait_send()
                    copy(mat, block, of_x, 3, to_x, 4).wait_send()

                each_block(far, one)

    start_of = pl.multiple_of(z * blk, 16)
    local = [
        pltpu.make_async_copy(tok, xs, local_sem.at[0]),
        pltpu.make_async_copy(w_up, weights.at[0, pl.ds(start_of, blk)], local_sem.at[1]),
        pltpu.make_async_copy(w_down_t, weights.at[1, pl.ds(start_of, blk)], local_sem.at[2]),
        pltpu.make_async_copy(w_neck, neck, local_sem.at[3]),
    ]
    for item in local:
        item.start()

    barrier = pltpu.get_barrier_semaphore()

    @pl.when(z < enc - 1)
    def _():
        pl.semaphore_signal(barrier, inc=1, device_id=up_z, device_id_type=MESH)

    @pl.when(z > 0)
    def _():
        pl.semaphore_signal(barrier, inc=1, device_id=down_z, device_id_type=MESH)

    pl.semaphore_signal(barrier, inc=1, device_id={"mp": 1 - m}, device_id_type=MESH)
    if split:
        pl.semaphore_signal(barrier, inc=1, device_id=to_x, device_id_type=MESH)
        pl.semaphore_signal(barrier, inc=1, device_id=to_y, device_id_type=MESH)
    peers = (3 if split else 1) + (z + enc - 1) // enc + 1 - (z + 1) // enc
    pl.semaphore_wait(barrier, peers)

    start_own(0)
    local[0].wait()
    rows = 32

    def first_norm(i, carry):
        at = pl.ds(pl.multiple_of(i * rows, rows), rows)
        normed[at, :] = layer_norm(xs[at, :].astype(jnp.float32), gain_pre[...]).astype(jnp.bfloat16)
        return carry

    lax.fori_loop(0, total // rows, first_norm, 0)

    far_all = range(1, enc)
    for far in far_all:
        if far == enc - 1:
            start_own(1)
        z_step(0, far)
        if far > 1:
            plane_step(0, far - 1)
    plane_step(0, enc - 1)
    early = max(1, enc - 2)
    for far in range(1, early):
        z_step(1, far)
    for far in far_all:
        diagonal_step(0, far)
    for far in range(early, enc - 1):
        z_step(1, far)
    local[1].wait()

    col_steps = ff // COLS
    units = col_steps * 2

    def up_unit(i, carry):
        at = pl.ds(pl.multiple_of((i % 2) * half, half), half)
        cols = pl.ds(pl.multiple_of((i // 2) * COLS, COLS), COLS)
        value = jnp.dot(normed[at, :], weights[0, :, cols], preferred_element_type=jnp.float32)
        value = 0.5 * value * (1.0 + lax.erf(value * 0.7071067811865476))
        hidden[at, cols] = value.astype(jnp.bfloat16)
        return carry

    edges = [units * i // 4 for i in range(5)]
    lax.fori_loop(edges[0], edges[1], up_unit, 0)
    z_step(1, enc - 1)
    for far in range(1, enc - 2):
        plane_step(1, far)
    lax.fori_loop(edges[1], edges[2], up_unit, 0)
    if enc > 2:
        plane_step(1, enc - 2)
    lax.fori_loop(edges[2], edges[3], up_unit, 0)
    plane_step(1, enc - 1)
    lax.fori_loop(edges[3], edges[4], up_unit, 0)
    for far in far_all:
        diagonal_step(1, far)
    local[2].wait()

    def down(first, dest, i):
        at = pl.ds(pl.multiple_of(first, half), half)
        cols = pl.ds(pl.multiple_of(i * COLS, COLS), COLS)
        value = lax.dot_general(
            hidden[at, :], weights[1, cols, :], (((1,), (1,)), ((), ())),
            preferred_element_type=jnp.float32,
        )
        dest[:, cols] = value.astype(jnp.bfloat16)

    def exchange(i):
        cols = pl.ds(pl.multiple_of(i * COLS, COLS), COLS)
        return pltpu.make_async_remote_copy(
            src_ref=give.at[:, cols], dst_ref=take.at[:, cols],
            send_sem=give_sem.at[i], recv_sem=take_sem.at[i],
            device_id={"mp": 1 - m}, device_id_type=MESH,
        )

    def other_half(i, carry):
        down((1 - m) * half, give, i)
        exchange(i).start()
        return carry

    def own_half(i, carry):
        down(m * half, own, i)
        return carry

    steps = width // COLS
    lax.fori_loop(0, steps, other_half, 0)
    lax.fori_loop(0, steps, own_half, 0)
    for i in range(steps):
        exchange(i).wait_recv()

    def second_norm(i, carry):
        at = pl.ds(pl.multiple_of(i * rows, rows), rows)
        whole = pl.ds(pl.multiple_of(m * half + i * rows, rows), rows)
        mixed = own[at, :].astype(jnp.float32) + take[at, :].astype(jnp.float32)
        value = xs[whole, :].astype(jnp.float32) + mixed
        normed[at, :] = layer_norm(value, gain_post[...]).astype(jnp.bfloat16)
        return carry

    lax.fori_loop(0, half // rows, second_norm, 0)
    local[3].wait()
    out[...] = jnp.dot(
        normed[0:half, :], neck[...], preferred_element_type=jnp.float32
    ).astype(jnp.bfloat16)

    finish_sends(0)
    finish_sends(1)
    for i in range(steps):
        exchange(i).wait_send()


def encoder(tokens, gain_pre, w_up, w_down, gain_post, w_neck):
    sizes = tuple(lax.axis_size(name) for name in ("groups", "enc", "dec"))
    enc = sizes[1]
    blk, ff = w_up.shape
    width = tokens.shape[-1]
    flat = tokens.reshape(-1, width)
    total = flat.shape[0]
    half = total // 2
    bf16 = jnp.bfloat16
    vmem = pl.BlockSpec(memory_space=pltpu.VMEM)
    anywhere = pl.BlockSpec(memory_space=pl.ANY)
    return pl.pallas_call(
        functools.partial(mlp_kernel, sizes),
        out_shape=jax.ShapeDtypeStruct((half, w_neck.shape[1]), bf16),
        in_specs=[anywhere, vmem, anywhere, anywhere, vmem, anywhere],
        out_specs=vmem,
        scratch_shapes=[
            pltpu.VMEM((2, width, ff), bf16),
            pltpu.VMEM((total, width), bf16),
            pltpu.VMEM((total, width), bf16),
            pltpu.VMEM((total, ff), bf16),
            pltpu.VMEM((half, width), bf16),
            pltpu.VMEM((half, width), bf16),
            pltpu.VMEM((half, width), bf16),
            pltpu.VMEM(w_neck.shape, bf16),
            pltpu.SemaphoreType.DMA((4,)),
            pltpu.SemaphoreType.DMA((2, enc, 4)),
            pltpu.SemaphoreType.DMA((2, enc, 5)),
            pltpu.SemaphoreType.DMA((width // COLS,)),
            pltpu.SemaphoreType.DMA((width // COLS,)),
        ],
        compiler_params=pltpu.CompilerParams(
            collective_id=0, has_side_effects=True, vmem_limit_bytes=48 * 1024 * 1024
        ),
    )(flat, gain_pre.reshape(1, -1), w_up, w_down.T, gain_post.reshape(1, -1), w_neck)


def body(
    tokens,
    gain_pre,
    w_up,
    w_down,
    gain_post,
    w_neck,
    conv_weight,
    conv_bias,
    cls_weight,
    cls_bias,
    tile_table,
    labels,
):
    enc_count = lax.axis_size("enc")
    mp_count = lax.axis_size("mp")
    enc_index = lax.axis_index("enc")
    mp_index = lax.axis_index("mp")
    slots = tokens.shape[1]
    side = tokens.shape[2]
    width = tokens.shape[4]
    row_groups = side // enc_count
    channels = w_neck.shape[1]
    table = tile_table[0]
    part = slots // mp_count
    own_entries = lax.dynamic_slice_in_dim(table, enc_index * slots + mp_index * part, part, 0)
    half_shift = jnp.maximum(own_entries[:, 0], 0) % side == side // 2
    values = encoder(tokens, gain_pre, w_up, w_down, gain_post, w_neck)
    values = values.reshape(part, side, side, channels)
    rolled = jnp.where(half_shift[:, None, None, None], jnp.roll(values, side // 2, axis=1), values)
    received = lax.all_to_all(
        rolled.reshape(part, row_groups, enc_count, side, channels),
        "enc",
        split_axis=2,
        concat_axis=2,
        tiled=True,
    )
    rows_local = labels.shape[0]
    band = labels.shape[2]
    entry_rows = table[:, 0]
    entry_cols = table[:, 1]
    shape_in = (part, row_groups, enc_count, side)
    group_ids = lax.broadcasted_iota(jnp.int32, shape_in, 1)
    col_ids = lax.broadcasted_iota(jnp.int32, shape_in, 3)
    here = lax.dynamic_slice_in_dim(table.reshape(enc_count, slots, 2), mp_index * part, part, 1)
    tab_rows = here[:, :, 0].T[:, None, :, None]
    tab_cols = here[:, :, 1].T[:, None, :, None]
    live_in = jnp.broadcast_to(tab_rows >= 0, shape_in)
    rolled_pos = group_ids * enc_count + enc_index
    tile_row = (rolled_pos - tab_rows) % side
    tile_col = col_ids
    target = (tab_rows + tile_row) // enc_count * band + tab_cols + tile_col
    target = jnp.where(live_in, target, -1)
    in_weight = jnp.where(
        live_in, blend_weight(tile_row.astype(jnp.float32), tile_col.astype(jnp.float32)), 0.0
    )
    positions = lax.broadcasted_iota(jnp.int32, (rows_local * band, in_weight.size), 0)
    spread_mat = jnp.where(
        positions == target.reshape(1, -1), in_weight.reshape(1, -1), 0.0
    ).astype(jnp.bfloat16)
    numer = jnp.dot(spread_mat, received.reshape(-1, channels), preferred_element_type=jnp.float32)
    numer = numer.astype(jnp.bfloat16)
    other = shifted(numer, "mp", 1)
    numer = numer.astype(jnp.float32) + other.astype(jnp.float32)
    strip_row = lax.broadcasted_iota(jnp.int32, (rows_local, band), 0) * enc_count + enc_index
    band_col = lax.broadcasted_iota(jnp.int32, (rows_local, band), 1)
    in_row = strip_row[None] - entry_rows[:, None, None]
    in_col = band_col[None] - entry_cols[:, None, None]
    inside = (
        (in_row >= 0)
        & (in_row < side)
        & (in_col >= 0)
        & (in_col < side)
        & (entry_rows >= 0)[:, None, None]
    )
    denom = jnp.sum(
        jnp.where(
            inside, blend_weight(in_row.astype(jnp.float32), in_col.astype(jnp.float32)), 0.0
        ),
        axis=0,
    )
    merged = (numer.reshape(rows_local, band, channels) / denom[:, :, None]).astype(jnp.bfloat16)
    above = shifted(merged, "enc", 1)
    below = shifted(merged, "enc", -1)
    zero_row = jnp.zeros_like(merged[:1])
    above = jnp.where(enc_index == 0, jnp.concatenate([zero_row, above[:-1]], 0), above)
    below = jnp.where(enc_index == enc_count - 1, jnp.concatenate([below[1:], zero_row], 0), below)
    stacked = jnp.stack([above, merged, below], 0)
    padded = padded_2(stacked, (("dec", 2),), 1)
    conv_sum = jnp.zeros((rows_local * band, conv_weight.shape[3]), jnp.float32)
    for row_off in range(3):
        for col_off in range(3):
            window = padded[row_off, :, col_off : col_off + band].reshape(-1, channels)
            conv_sum = conv_sum + jnp.dot(
                window, conv_weight[row_off, col_off], preferred_element_type=jnp.float32
            )
    activ = jax.nn.relu(conv_sum + conv_bias).astype(jnp.bfloat16)
    partial_logits = jnp.dot(activ, cls_weight, preferred_element_type=jnp.float32)
    logits = lax.psum(partial_logits, "mp") + cls_bias
    logits = logits.reshape(rows_local, 1, band, logits.shape[-1])
    classes = lax.broadcasted_iota(jnp.int32, (1, 1, 1, logits.shape[-1]), 3)
    picked = jnp.sum(jnp.where(labels[..., None] == classes, logits, 0.0), axis=-1)
    nll = jnp.log(jnp.sum(jnp.exp(logits), axis=-1)) - picked
    return (logits, nll)


def solution(mesh):
    in_specs = (
        P(("groups", "dec"), "enc", None, None, None),
        P(),
        P("enc", "mp"),
        P("mp", "enc"),
        P(),
        P(),
        P(None, None, None, "mp"),
        P("mp"),
        P("mp", None),
        P(),
        P(("groups", "dec"), None, None),
        P(None, "enc", ("groups", "dec")),
    )
    out_specs = (P(None, "enc", ("groups", "dec"), None), P(None, "enc", ("groups", "dec")))
    return jax.shard_map(body, mesh=mesh, in_specs=in_specs, out_specs=out_specs, check_vma=False)
```

```python
import functools

import jax
import jax.numpy as jnp
from jax import lax
from jax.experimental import pallas as pl
from jax.experimental.pallas import tpu as pltpu
from jax.sharding import PartitionSpec as P

TS = 16


norm_eps = 1e-05
blend_sigma = 4.0


def layer_norm(values, scale_vec):
    row_mean = jnp.mean(values, axis=-1, keepdims=True)
    centered = values - row_mean
    row_var = jnp.mean(centered * centered, axis=-1, keepdims=True)
    return centered * lax.rsqrt(row_var + norm_eps) * scale_vec


MESH = pl.DeviceIdType.MESH
COLS = 256


def strip_kernel(
    sizes, sizes_rows, tok, gain_pre, w_up, w_down_t, gain_post, w_neck, conv_hbm, conv_bias, cls_t, table,
    out,
    weights, xs, normed, hidden, give, take, own, neck,
    conv_w, deal, dealt, spread, denom, part_sum, other_sum, merged, halo, edge, edges_in,
    part_logits, other_logits,
    local_sem, recv_sem, send_sem, give_sem, take_sem,
    deal_send, deal_recv, pair_send, pair_recv, halo_send, halo_recv, edge_send, edge_recv,
):
    groups, enc, dec = sizes
    y, z = lax.axis_index("groups"), lax.axis_index("enc")
    x, m = lax.axis_index("dec"), lax.axis_index("mp")
    blk, ff = w_up.shape
    total, width = xs.shape
    spread_rows = sizes_rows
    half = total // 2
    split = groups % 2 == 0 and dec % 2 == 0 and blk % 64 == 0
    parts = 4 if split else 1
    piece = blk // parts
    ox, oy = x + 1 - 2 * (x % 2), y + 1 - 2 * (y % 2)
    mine = (y % 2) * 2 + x % 2 if split else 0
    of_x = (y % 2) * 2 + 1 - x % 2
    of_y = (1 - y % 2) * 2 + x % 2
    diagonal = (1 - y % 2) * 2 + 1 - x % 2

    def region(mat, block, quarter):
        start = pl.multiple_of(block * blk + quarter * piece, 16)
        return weights.at[mat, pl.ds(start, piece)]

    def copy(mat, block, quarter, kind, target, sent, own_src=False):
        dst = region(mat, block, quarter)
        src = dst
        if own_src:
            start = pl.multiple_of(quarter * piece, 16)
            src = (w_up, w_down_t)[mat].at[pl.ds(start, piece)]
        return pltpu.make_async_remote_copy(
            src_ref=src, dst_ref=dst,
            send_sem=send_sem.at[mat, block, sent], recv_sem=recv_sem.at[mat, block, kind],
            device_id=target, device_id_type=MESH,
        )

    up_z, down_z = {"enc": z + 1}, {"enc": z - 1}
    to_x, to_y = {"dec": ox}, {"groups": oy}

    def own_sends(mat):
        right = copy(mat, z, mine, 0, up_z, 0, True)
        left = copy(mat, z, mine, 0, down_z, 1, True)
        return right, left

    def start_own(mat):
        right, left = own_sends(mat)

        @pl.when(z < enc - 1)
        def _():
            right.start()

        @pl.when(z > 0)
        def _():
            left.start()

    def z_step(mat, far):
        @pl.when(z - far >= 0)
        def _():
            block = z - far
            copy(mat, block, mine, 0, up_z, 0).wait_recv()

            @pl.when(z < enc - 1)
            def _():
                copy(mat, block, mine, 0, up_z, 0).start()

            if split:
                copy(mat, block, mine, 1, to_x, 2).start()
                copy(mat, block, mine, 2, to_y, 3).start()

        @pl.when(z + far < enc)
        def _():
            block = z + far
            copy(mat, block, mine, 0, down_z, 1).wait_recv()

            @pl.when(z > 0)
            def _():
                copy(mat, block, mine, 0, down_z, 1).start()

            if split:
                copy(mat, block, mine, 1, to_x, 2).start()
                copy(mat, block, mine, 2, to_y, 3).start()

    def each_block(far, fn):
        @pl.when(z - far >= 0)
        def _():
            fn(z - far)

        @pl.when(z + far < enc)
        def _():
            fn(z + far)

    def plane_step(mat, far):
        if not split:
            return

        def one(block):
            by_y = (block + mat) % 2 == 0
            copy(mat, block, of_x, 1, to_x, 2).wait_recv()

            @pl.when(by_y)
            def _():
                copy(mat, block, of_x, 3, to_y, 4).start()

            copy(mat, block, of_y, 2, to_y, 3).wait_recv()

            @pl.when(jnp.logical_not(by_y))
            def _():
                copy(mat, block, of_y, 3, to_x, 4).start()

        each_block(far, one)

    def diagonal_step(mat, far):
        if split:
            each_block(far, lambda block: copy(mat, block, diagonal, 3, to_x, 4).wait_recv())

    def finish_sends(mat):
        right, left = own_sends(mat)

        @pl.when(z < enc - 1)
        def _():
            right.wait_send()

        @pl.when(z > 0)
        def _():
            left.wait_send()

        for far in range(1, enc):
            @pl.when((z - far >= 0) & (z < enc - 1))
            def _(far=far):
                copy(mat, z - far, mine, 0, up_z, 0).wait_send()

            @pl.when((z + far < enc) & (z > 0))
            def _(far=far):
                copy(mat, z + far, mine, 0, down_z, 1).wait_send()

            if split:
                def one(block):
                    copy(mat, block, mine, 1, to_x, 2).wait_send()
                    copy(mat, block, mine, 2, to_y, 3).wait_send()
                    copy(mat, block, of_x, 3, to_x, 4).wait_send()

                each_block(far, one)

    start_of = pl.multiple_of(z * blk, 16)
    local = [
        pltpu.make_async_copy(tok, xs, local_sem.at[0]),
        pltpu.make_async_copy(w_up, weights.at[0, pl.ds(start_of, blk)], local_sem.at[1]),
        pltpu.make_async_copy(w_down_t, weights.at[1, pl.ds(start_of, blk)], local_sem.at[2]),
        pltpu.make_async_copy(w_neck, neck, local_sem.at[3]),
        pltpu.make_async_copy(conv_hbm, conv_w, local_sem.at[4]),
    ]
    for item in local:
        item.start()

    edges_in[...] = jnp.zeros_like(edges_in)
    above_z, below_z = (z + enc - 1) % enc, (z + 1) % enc
    barrier = pltpu.get_barrier_semaphore()

    def greet(**target):
        pl.semaphore_signal(barrier, inc=1, device_id=target, device_id_type=MESH)

    for off in range(1, enc):
        greet(enc=(z + off) % enc)
    greet(mp=1 - m)
    if split:
        greet(groups=oy)

    def greet_side(side_x):
        greet(dec=side_x)
        greet(dec=side_x, enc=above_z)
        greet(dec=side_x, enc=below_z)

    @pl.when(x > 0)
    def _():
        greet_side(x - 1)

    @pl.when(x < dec - 1)
    def _():
        greet_side(x + 1)

    sides = (x + dec - 1) // dec + 1 - (x + 1) // dec
    pl.semaphore_wait(barrier, enc + (1 if split else 0) + 3 * sides)

    start_own(0)
    local[0].wait()
    rows = 32

    def first_norm(i, carry):
        at = pl.ds(pl.multiple_of(i * rows, rows), rows)
        normed[at, :] = layer_norm(xs[at, :].astype(jnp.float32), gain_pre[...]).astype(jnp.bfloat16)
        return carry

    lax.fori_loop(0, total // rows, first_norm, 0)

    side = TS
    slots = total // (side * side)
    part = slots // 2
    row_groups = side // enc
    run = row_groups * side
    band = denom.shape[0] // spread_rows
    places = spread_rows * band
    lanes = enc * part * run
    lane = lax.broadcasted_iota(jnp.int32, (1, lanes), 1)
    strip_row = lax.broadcasted_iota(jnp.int32, (spread_rows, band, lanes), 0) * enc + z
    strip_row = strip_row.reshape(places, lanes)
    band_col = lax.broadcasted_iota(jnp.int32, (spread_rows, band, lanes), 1).reshape(places, lanes)

    def spread_of(owner):
        top = jnp.zeros((1, lanes), jnp.int32)
        left = jnp.zeros((1, lanes), jnp.int32)
        group = jnp.zeros((1, lanes), jnp.int32)
        col = lane
        for unit in range(enc * part):
            entry = (unit // part) * slots + owner * part + unit % part
            inside = lane >= unit * run
            top = jnp.where(inside, table[0, 0, entry], top)
            left = jnp.where(inside, table[0, 1, entry], left)
            for g in range(row_groups):
                begin = lane >= unit * run + g * side
                group = jnp.where(begin, g, group)
                col = jnp.where(begin, lane - (unit * run + g * side), col)
        tile_row = jnp.bitwise_and(group * enc + z - top, side - 1)
        middle = (side - 1) / 2.0
        dr = tile_row.astype(jnp.float32) - middle
        dc = col.astype(jnp.float32) - middle
        weight = jnp.exp(-(dr * dr + dc * dc) / (2.0 * blend_sigma * blend_sigma))
        weight = weight.astype(jnp.bfloat16).astype(jnp.float32)
        weight = jnp.where(top >= 0, weight, 0.0)
        hit = (strip_row == top + tile_row) & (band_col == left + col)
        return jnp.where(hit, weight, 0.0)

    mine_spread = spread_of(m)
    spread[...] = mine_spread.astype(jnp.bfloat16)
    denom[...] = jnp.sum(mine_spread + spread_of(1 - m), axis=1, keepdims=True)

    far_all = range(1, enc)
    for far in far_all:
        if far == enc - 1:
            start_own(1)
        z_step(0, far)
        if far > 1:
            plane_step(0, far - 1)
    plane_step(0, enc - 1)
    early = max(1, enc - 2)
    for far in range(1, early):
        z_step(1, far)
    for far in far_all:
        diagonal_step(0, far)
    for far in range(early, enc - 1):
        z_step(1, far)
    local[1].wait()

    col_steps = ff // COLS
    units = col_steps * 2

    def up_unit(i, carry):
        at = pl.ds(pl.multiple_of((i % 2) * half, half), half)
        cols = pl.ds(pl.multiple_of((i // 2) * COLS, COLS), COLS)
        value = jnp.dot(normed[at, :], weights[0, :, cols], preferred_element_type=jnp.float32)
        value = 0.5 * value * (1.0 + lax.erf(value * 0.7071067811865476))
        hidden[at, cols] = value.astype(jnp.bfloat16)
        return carry

    edges = [units * i // 4 for i in range(5)]
    lax.fori_loop(edges[0], edges[1], up_unit, 0)
    z_step(1, enc - 1)
    for far in range(1, enc - 2):
        plane_step(1, far)
    lax.fori_loop(edges[1], edges[2], up_unit, 0)
    if enc > 2:
        plane_step(1, enc - 2)
    lax.fori_loop(edges[2], edges[3], up_unit, 0)
    plane_step(1, enc - 1)
    lax.fori_loop(edges[3], edges[4], up_unit, 0)
    for far in far_all:
        diagonal_step(1, far)
    local[2].wait()

    def down(first, dest, i):
        at = pl.ds(pl.multiple_of(first, half), half)
        cols = pl.ds(pl.multiple_of(i * COLS, COLS), COLS)
        value = lax.dot_general(
            hidden[at, :], weights[1, cols, :], (((1,), (1,)), ((), ())),
            preferred_element_type=jnp.float32,
        )
        dest[:, cols] = value.astype(jnp.bfloat16)

    def exchange(i):
        cols = pl.ds(pl.multiple_of(i * COLS, COLS), COLS)
        return pltpu.make_async_remote_copy(
            src_ref=give.at[:, cols], dst_ref=take.at[:, cols],
            send_sem=give_sem.at[i], recv_sem=take_sem.at[i],
            device_id={"mp": 1 - m}, device_id_type=MESH,
        )

    def other_half(i, carry):
        down((1 - m) * half, give, i)
        exchange(i).start()
        return carry

    def own_half(i, carry):
        down(m * half, own, i)
        return carry

    steps = width // COLS
    lax.fori_loop(0, steps, other_half, 0)
    lax.fori_loop(0, steps, own_half, 0)
    for i in range(steps):
        exchange(i).wait_recv()

    def second_norm(i, carry):
        at = pl.ds(pl.multiple_of(i * rows, rows), rows)
        whole = pl.ds(pl.multiple_of(m * half + i * rows, rows), rows)
        mixed = own[at, :].astype(jnp.float32) + take[at, :].astype(jnp.float32)
        value = xs[whole, :].astype(jnp.float32) + mixed
        normed[at, :] = layer_norm(value, gain_post[...]).astype(jnp.bfloat16)
        return carry

    lax.fori_loop(0, half // rows, second_norm, 0)
    local[3].wait()
    values = jnp.dot(
        normed[0:half, :], neck[...], preferred_element_type=jnp.float32
    ).astype(jnp.bfloat16)
    tile_size = side * side
    for slot in range(part):
        value = values[slot * tile_size : (slot + 1) * tile_size]
        top = table[0, 0, z * slots + m * part + slot]
        swapped = jnp.concatenate([value[tile_size // 2 :], value[: tile_size // 2]], axis=0)
        flag = jnp.bitwise_and(jnp.maximum(top, 0), side - 1) == side // 2
        value = jnp.where(flag, swapped.astype(jnp.float32), value.astype(jnp.float32)).astype(jnp.bfloat16)
        for row in range(side):
            at = slot * run + (row // enc) * side
            deal[row % enc, at : at + side, :] = value[row * side : (row + 1) * side]

    def deal_copy(off):
        target = (z + off) % enc
        return pltpu.make_async_remote_copy(
            src_ref=deal.at[target], dst_ref=dealt.at[z],
            send_sem=deal_send.at[off], recv_sem=deal_recv.at[off],
            device_id={"enc": target}, device_id_type=MESH,
        )

    for off in range(1, enc):
        deal_copy(off).start()
    dealt[z] = deal[z]
    local[4].wait()
    for off in range(1, enc):
        deal_copy(off).wait_recv()
    channels = deal.shape[2]
    numer = jnp.dot(
        spread[...], dealt[...].reshape(lanes, channels), preferred_element_type=jnp.float32
    )
    part_sum[...] = numer.astype(jnp.bfloat16)

    def pair(src, dst, which):
        return pltpu.make_async_remote_copy(
            src_ref=src, dst_ref=dst, send_sem=pair_send.at[which], recv_sem=pair_recv.at[which],
            device_id={"mp": 1 - m}, device_id_type=MESH,
        )

    swap_sum = pair(part_sum, other_sum, 0)
    swap_sum.start()
    swap_sum.wait_recv()
    numer = part_sum[...].astype(jnp.float32) + other_sum[...].astype(jnp.float32)
    whole = numer / denom[...]
    merged[...] = whole.astype(jnp.bfloat16)

    def halo_copy(which):
        return pltpu.make_async_remote_copy(
            src_ref=merged, dst_ref=halo.at[which],
            send_sem=halo_send.at[which], recv_sem=halo_recv.at[which],
            device_id={"enc": (below_z, above_z)[which]}, device_id_type=MESH,
        )

    halo_copy(0).start()
    halo_copy(1).start()
    cube = whole.reshape(spread_rows, band, channels)
    blank = jnp.zeros((edge.shape[1] - spread_rows, channels), jnp.float32)
    edge[0] = jnp.concatenate([cube[:, 0, :], blank], axis=0).astype(jnp.bfloat16)
    edge[1] = jnp.concatenate([cube[:, band - 1, :], blank], axis=0).astype(jnp.bfloat16)

    def edge_copy(which, level):
        target = {"dec": (x - 1, x + 1)[which]}
        if level:
            target["enc"] = (below_z, above_z)[level - 1]
        return pltpu.make_async_remote_copy(
            src_ref=edge.at[which], dst_ref=edges_in.at[1 - which, level],
            send_sem=edge_send.at[which, level], recv_sem=edge_recv.at[1 - which, level],
            device_id=target, device_id_type=MESH,
        )

    def every_edge(which, act):
        @pl.when((x > 0) if which == 0 else (x < dec - 1))
        def _():
            for level in range(3):
                act(edge_copy(which, level))

    every_edge(0, lambda c: c.start())
    every_edge(1, lambda c: c.start())

    kinds = conv_w.shape[3]

    def products(source, row_off):
        return [
            jnp.dot(source, conv_w[row_off, b], preferred_element_type=jnp.float32) for b in range(3)
        ]

    spot = lax.broadcasted_iota(jnp.int32, (spread_rows, band, kinds), 0).reshape(places, kinds)
    spot_col = lax.broadcasted_iota(jnp.int32, (spread_rows, band, kinds), 1).reshape(places, kinds)
    center = products(merged[...], 1)

    def moved_down(value, step, index):
        shifted_value = jnp.where(index == 0, 0.0, pltpu.roll(value, step, 0))
        return jnp.where(z == 0, shifted_value, value)

    def moved_up(value, step, index):
        size = value.shape[0]
        shifted_value = jnp.where(index == spread_rows - 1, 0.0, pltpu.roll(value, size - step, 0))
        return jnp.where(z == enc - 1, shifted_value, value)

    halo_copy(0).wait_recv()
    upper = products(halo[0], 0)
    halo_copy(1).wait_recv()
    lower = products(halo[1], 2)
    for which in range(2):
        every_edge(1 - which, lambda c: c.wait_send())

    @pl.when(x < dec - 1)
    def _():
        for level in range(3):
            edge_copy(0, level).wait_recv()

    @pl.when(x > 0)
    def _():
        for level in range(3):
            edge_copy(1, level).wait_recv()

    sums = [
        center[b] + moved_down(upper[b], band, spot) + moved_up(lower[b], band, spot) for b in range(3)
    ]
    index = lax.broadcasted_iota(jnp.int32, (edge.shape[1], kinds), 0)

    def edge_sum(which, b):
        levels = [
            jnp.dot(edges_in[which, level], conv_w[a, b], preferred_element_type=jnp.float32)
            for level, a in ((0, 1), (1, 0), (2, 2))
        ]
        value = levels[0] + moved_down(levels[1], 1, index) + moved_up(levels[2], 1, index)
        value = value[:spread_rows].reshape(spread_rows, 1, kinds)
        return jnp.broadcast_to(value, (spread_rows, band, kinds)).reshape(places, kinds)

    before = jnp.where(spot_col == 0, edge_sum(0, 0), pltpu.roll(sums[0], 1, 0))
    after = jnp.where(spot_col == band - 1, edge_sum(1, 2), pltpu.roll(sums[2], places - 1, 0))
    activ = jnp.maximum(sums[1] + before + after + conv_bias[...], 0.0).astype(jnp.bfloat16)
    part_logits[...] = lax.dot_general(
        cls_t[...], activ, (((1,), (1,)), ((), ())), preferred_element_type=jnp.float32
    )
    swap_logits = pair(part_logits, other_logits, 1)
    swap_logits.start()
    swap_logits.wait_recv()
    out[...] = part_logits[...] + other_logits[...]

    swap_sum.wait_send()
    swap_logits.wait_send()
    halo_copy(0).wait_send()
    halo_copy(1).wait_send()
    for off in range(1, enc):
        deal_copy(off).wait_send()
    finish_sends(0)
    finish_sends(1)
    for i in range(steps):
        exchange(i).wait_send()


def body(
    tokens,
    gain_pre,
    w_up,
    w_down,
    gain_post,
    w_neck,
    conv_weight,
    conv_bias,
    cls_weight,
    cls_bias,
    tile_table,
    labels,
):
    sizes = tuple(lax.axis_size(name) for name in ("groups", "enc", "dec"))
    enc = sizes[1]
    blk, ff = w_up.shape
    width = tokens.shape[-1]
    flat = tokens.reshape(-1, width)
    total = flat.shape[0]
    half = total // 2
    rows_local, _, band = labels.shape
    places = rows_local * band
    channels = w_neck.shape[1]
    classes = cls_weight.shape[1]
    dealt_rows = half // enc
    edge_rows = -(-rows_local // 16) * 16
    bf16, f32 = jnp.bfloat16, jnp.float32
    vmem = pl.BlockSpec(memory_space=pltpu.VMEM)
    anywhere = pl.BlockSpec(memory_space=pl.ANY)
    dma = pltpu.SemaphoreType.DMA
    sums = pl.pallas_call(
        functools.partial(strip_kernel, sizes, rows_local),
        out_shape=jax.ShapeDtypeStruct((classes, places), f32),
        in_specs=[anywhere, vmem, anywhere, anywhere, vmem, anywhere, anywhere, vmem, vmem,
                  pl.BlockSpec(memory_space=pltpu.SMEM)],
        out_specs=vmem,
        scratch_shapes=[
            pltpu.VMEM((2, width, ff), bf16),
            pltpu.VMEM((total, width), bf16),
            pltpu.VMEM((total, width), bf16),
            pltpu.VMEM((total, ff), bf16),
            pltpu.VMEM((half, width), bf16),
            pltpu.VMEM((half, width), bf16),
            pltpu.VMEM((half, width), bf16),
            pltpu.VMEM(w_neck.shape, bf16),
            pltpu.VMEM(conv_weight.shape, bf16),
            pltpu.VMEM((enc, dealt_rows, channels), bf16),
            pltpu.VMEM((enc, dealt_rows, channels), bf16),
            pltpu.VMEM((places, half), bf16),
            pltpu.VMEM((places, 1), f32),
            pltpu.VMEM((places, channels), bf16),
            pltpu.VMEM((places, channels), bf16),
            pltpu.VMEM((places, channels), bf16),
            pltpu.VMEM((2, places, channels), bf16),
            pltpu.VMEM((2, edge_rows, channels), bf16),
            pltpu.VMEM((2, 3, edge_rows, channels), bf16),
            pltpu.VMEM((classes, places), f32),
            pltpu.VMEM((classes, places), f32),
            dma((5,)),
            dma((2, enc, 4)),
            dma((2, enc, 5)),
            dma((width // COLS,)),
            dma((width // COLS,)),
            dma((enc,)),
            dma((enc,)),
            dma((2,)),
            dma((2,)),
            dma((2,)),
            dma((2,)),
            dma((2, 3)),
            dma((2, 3)),
        ],
        compiler_params=pltpu.CompilerParams(
            collective_id=0, has_side_effects=True, vmem_limit_bytes=60 * 1024 * 1024
        ),
    )(
        flat, gain_pre.reshape(1, -1), w_up, w_down.T, gain_post.reshape(1, -1), w_neck,
        conv_weight, conv_bias.reshape(1, -1), cls_weight.T, jnp.swapaxes(tile_table, 1, 2),
    )
    logits = sums.T + cls_bias
    logits = logits.reshape(rows_local, 1, band, classes)
    ids = lax.broadcasted_iota(jnp.int32, (1, 1, 1, classes), 3)
    picked = jnp.sum(jnp.where(labels[..., None] == ids, logits, 0.0), axis=-1)
    nll = jnp.log(jnp.sum(jnp.exp(logits), axis=-1)) - picked
    return (logits, nll)


def solution(mesh):
    in_specs = (
        P(("groups", "dec"), "enc", None, None, None),
        P(),
        P("enc", "mp"),
        P("mp", "enc"),
        P(),
        P(),
        P(None, None, None, "mp"),
        P("mp"),
        P("mp", None),
        P(),
        P(("groups", "dec"), None, None),
        P(None, "enc", ("groups", "dec")),
    )
    out_specs = (P(None, "enc", ("groups", "dec"), None), P(None, "enc", ("groups", "dec")))
    return jax.shard_map(body, mesh=mesh, in_specs=in_specs, out_specs=out_specs, check_vma=False)
```

```python
import functools

import jax
import jax.numpy as jnp
from jax import lax
from jax.experimental import pallas as pl
from jax.experimental.pallas import tpu as pltpu
from jax.sharding import PartitionSpec as P

TS = 16


norm_eps = 1e-05
blend_sigma = 4.0


def layer_norm(values, scale_vec):
    row_mean = jnp.mean(values, axis=-1, keepdims=True)
    centered = values - row_mean
    row_var = jnp.mean(centered * centered, axis=-1, keepdims=True)
    return centered * lax.rsqrt(row_var + norm_eps) * scale_vec


MESH = pl.DeviceIdType.MESH
COLS = 256


def strip_kernel(
    sizes, sizes_rows, tok, gain_pre, w_up, w_down_t, gain_post, w_neck, conv_hbm, conv_bias, cls_t, table,
    cls_bias, labels, out, out_nll,
    gains, weights, xs, normed, hidden, give, take, own, neck,
    conv_w, deal, dealt, spread, denom, part_sum, other_sum, merged, halo, edge, edges_in,
    part_logits, other_logits,
    local_sem, recv_sem, send_sem, give_sem, take_sem,
    deal_send, deal_recv, pair_send, pair_recv, halo_send, halo_recv, edge_send, edge_recv,
):
    groups, enc, dec = sizes
    y, z = lax.axis_index("groups"), lax.axis_index("enc")
    x, m = lax.axis_index("dec"), lax.axis_index("mp")
    blk, ff = w_up.shape
    total, width = xs.shape
    spread_rows = sizes_rows
    half = total // 2
    split = groups % 2 == 0 and dec % 2 == 0 and blk % 64 == 0
    parts = 4 if split else 1
    piece = blk // parts
    ox, oy = x + 1 - 2 * (x % 2), y + 1 - 2 * (y % 2)
    mine = (y % 2) * 2 + x % 2 if split else 0
    of_x = (y % 2) * 2 + 1 - x % 2
    of_y = (1 - y % 2) * 2 + x % 2
    diagonal = (1 - y % 2) * 2 + 1 - x % 2

    def region(mat, block, quarter):
        start = pl.multiple_of(block * blk + quarter * piece, 16)
        return weights.at[mat, pl.ds(start, piece)]

    def copy(mat, block, quarter, kind, target, sent, own_src=False):
        dst = region(mat, block, quarter)
        src = dst
        if own_src:
            start = pl.multiple_of(quarter * piece, 16)
            src = (w_up, w_down_t)[mat].at[pl.ds(start, piece)]
        return pltpu.make_async_remote_copy(
            src_ref=src, dst_ref=dst,
            send_sem=send_sem.at[mat, block, sent], recv_sem=recv_sem.at[mat, block, kind],
            device_id=target, device_id_type=MESH,
        )

    up_z, down_z = {"enc": z + 1}, {"enc": z - 1}
    to_x, to_y = {"dec": ox}, {"groups": oy}

    def own_sends(mat):
        right = copy(mat, z, mine, 0, up_z, 0, True)
        left = copy(mat, z, mine, 0, down_z, 1, True)
        if not split:
            return (right,), (left,)
        right_diagonal = copy(mat, z, diagonal, 3, up_z, 4, True)
        left_diagonal = copy(mat, z, diagonal, 3, down_z, 5, True)
        return (right, right_diagonal), (left, left_diagonal)

    def start_own(mat):
        right, left = own_sends(mat)

        @pl.when(z < enc - 1)
        def _():
            for item in right:
                item.start()

        @pl.when(z > 0)
        def _():
            for item in left:
                item.start()

    def z_step(mat, far):
        @pl.when(z - far >= 0)
        def _():
            block = z - far
            copy(mat, block, mine, 0, up_z, 0).wait_recv()

            @pl.when(z < enc - 1)
            def _():
                copy(mat, block, mine, 0, up_z, 0).start()

            if split:
                copy(mat, block, mine, 1, to_x, 2).start()
                copy(mat, block, mine, 2, to_y, 3).start()

        @pl.when(z + far < enc)
        def _():
            block = z + far
            copy(mat, block, mine, 0, down_z, 1).wait_recv()

            @pl.when(z > 0)
            def _():
                copy(mat, block, mine, 0, down_z, 1).start()

            if split:
                copy(mat, block, mine, 1, to_x, 2).start()
                copy(mat, block, mine, 2, to_y, 3).start()

    def each_block(far, fn):
        @pl.when(z - far >= 0)
        def _():
            fn(z - far)

        @pl.when(z + far < enc)
        def _():
            fn(z + far)

    def plane_step(mat, far):
        if not split:
            return

        def one(block):
            by_y = (block + mat) % 2 == 0
            copy(mat, block, of_x, 1, to_x, 2).wait_recv()

            if far > 1:
                @pl.when(by_y)
                def _():
                    copy(mat, block, of_x, 3, to_y, 4).start()

            copy(mat, block, of_y, 2, to_y, 3).wait_recv()

            if far > 1:
                @pl.when(jnp.logical_not(by_y))
                def _():
                    copy(mat, block, of_y, 3, to_x, 4).start()

        each_block(far, one)

    def diagonal_step(mat, far):
        if split:
            each_block(far, lambda block: copy(mat, block, diagonal, 3, to_x, 4).wait_recv())

    def finish_sends(mat):
        right, left = own_sends(mat)

        @pl.when(z < enc - 1)
        def _():
            for item in right:
                item.wait_send()

        @pl.when(z > 0)
        def _():
            for item in left:
                item.wait_send()

        for far in range(1, enc):
            @pl.when((z - far >= 0) & (z < enc - 1))
            def _(far=far):
                copy(mat, z - far, mine, 0, up_z, 0).wait_send()

            @pl.when((z + far < enc) & (z > 0))
            def _(far=far):
                copy(mat, z + far, mine, 0, down_z, 1).wait_send()

            if split:
                def one(block, far=far):
                    copy(mat, block, mine, 1, to_x, 2).wait_send()
                    copy(mat, block, mine, 2, to_y, 3).wait_send()
                    if far > 1:
                        copy(mat, block, of_x, 3, to_x, 4).wait_send()

                each_block(far, one)

    start_of = pl.multiple_of(z * blk, 16)
    local = [
        pltpu.make_async_copy(tok, xs, local_sem.at[0]),
        pltpu.make_async_copy(w_up, weights.at[0, pl.ds(start_of, blk)], local_sem.at[1]),
        pltpu.make_async_copy(w_down_t, weights.at[1, pl.ds(start_of, blk)], local_sem.at[2]),
        pltpu.make_async_copy(w_neck, neck, local_sem.at[3]),
        pltpu.make_async_copy(conv_hbm, conv_w, local_sem.at[4]),
    ]
    for item in local:
        item.start()

    edges_in[...] = jnp.zeros_like(edges_in)
    above_z, below_z = (z + enc - 1) % enc, (z + 1) % enc
    barrier = pltpu.get_barrier_semaphore()

    def greet(**target):
        pl.semaphore_signal(barrier, inc=1, device_id=target, device_id_type=MESH)

    for off in range(1, enc):
        greet(enc=(z + off) % enc)
    greet(mp=1 - m)
    if split:
        greet(groups=oy)

    def greet_side(side_x):
        greet(dec=side_x)
        greet(dec=side_x, enc=above_z)
        greet(dec=side_x, enc=below_z)

    @pl.when(x > 0)
    def _():
        greet_side(x - 1)

    @pl.when(x < dec - 1)
    def _():
        greet_side(x + 1)

    sides = (x + dec - 1) // dec + 1 - (x + 1) // dec
    pl.semaphore_wait(barrier, enc + (1 if split else 0) + 3 * sides)

    start_own(0)
    local[0].wait()
    rows = 32

    def wide(ref):
        return jnp.concatenate([ref[i : i + 1, :] for i in range(ref.shape[0])], axis=1)

    gains[0:1, :] = wide(gain_pre)
    gains[1:2, :] = wide(gain_post)

    def first_norm(i, carry):
        at = pl.ds(pl.multiple_of(i * rows, rows), rows)
        normed[at, :] = layer_norm(xs[at, :].astype(jnp.float32), gains[0:1, :]).astype(jnp.bfloat16)
        return carry

    lax.fori_loop(0, total // rows, first_norm, 0)

    side = TS
    slots = total // (side * side)
    part = slots // 2
    row_groups = side // enc
    run = row_groups * side
    band = denom.shape[0] // spread_rows
    places = spread_rows * band
    lanes = enc * part * run
    lane = lax.broadcasted_iota(jnp.int32, (1, lanes), 1)
    strip_row = lax.broadcasted_iota(jnp.int32, (spread_rows, band, lanes), 0) * enc + z
    strip_row = strip_row.reshape(places, lanes)
    band_col = lax.broadcasted_iota(jnp.int32, (spread_rows, band, lanes), 1).reshape(places, lanes)

    def spread_of(owner):
        top = jnp.zeros((1, lanes), jnp.int32)
        left = jnp.zeros((1, lanes), jnp.int32)
        group = jnp.zeros((1, lanes), jnp.int32)
        col = lane
        for unit in range(enc * part):
            entry = (unit // part) * slots + owner * part + unit % part
            inside = lane >= unit * run
            top = jnp.where(inside, table[0, 0, entry], top)
            left = jnp.where(inside, table[0, 1, entry], left)
            for g in range(row_groups):
                begin = lane >= unit * run + g * side
                group = jnp.where(begin, g, group)
                col = jnp.where(begin, lane - (unit * run + g * side), col)
        tile_row = jnp.bitwise_and(group * enc + z - top, side - 1)
        middle = (side - 1) / 2.0
        dr = tile_row.astype(jnp.float32) - middle
        dc = col.astype(jnp.float32) - middle
        weight = jnp.exp(-(dr * dr + dc * dc) / (2.0 * blend_sigma * blend_sigma))
        weight = weight.astype(jnp.bfloat16).astype(jnp.float32)
        weight = jnp.where(top >= 0, weight, 0.0)
        hit = (strip_row == top + tile_row) & (band_col == left + col)
        return jnp.where(hit, weight, 0.0)

    mine_spread = spread_of(m)
    spread[...] = mine_spread.astype(jnp.bfloat16)
    denom[...] = jnp.sum(mine_spread + spread_of(1 - m), axis=1, keepdims=True)

    far_all = range(1, enc)
    for far in far_all:
        if far == enc - 1:
            start_own(1)
        z_step(0, far)
        if far > 1:
            plane_step(0, far - 1)
    plane_step(0, enc - 1)
    early = max(1, enc - 2)
    for far in range(1, early):
        z_step(1, far)
    for far in far_all:
        diagonal_step(0, far)
    for far in range(early, enc - 1):
        z_step(1, far)
    local[1].wait()

    col_steps = ff // COLS
    units = col_steps * 2

    def up_unit(i, carry):
        at = pl.ds(pl.multiple_of((i % 2) * half, half), half)
        cols = pl.ds(pl.multiple_of((i // 2) * COLS, COLS), COLS)
        value = jnp.dot(normed[at, :], weights[0, :, cols], preferred_element_type=jnp.float32)
        value = 0.5 * value * (1.0 + lax.erf(value * 0.7071067811865476))
        hidden[at, cols] = value.astype(jnp.bfloat16)
        return carry

    edges = [units * i // 4 for i in range(5)]
    lax.fori_loop(edges[0], edges[1], up_unit, 0)
    z_step(1, enc - 1)
    for far in range(1, enc - 2):
        plane_step(1, far)
    lax.fori_loop(edges[1], edges[2], up_unit, 0)
    if enc > 2:
        plane_step(1, enc - 2)
    lax.fori_loop(edges[2], edges[3], up_unit, 0)
    plane_step(1, enc - 1)
    lax.fori_loop(edges[3], edges[4], up_unit, 0)
    for far in far_all:
        diagonal_step(1, far)
    local[2].wait()

    def down(first, dest, i):
        at = pl.ds(pl.multiple_of(first, half), half)
        cols = pl.ds(pl.multiple_of(i * COLS, COLS), COLS)
        value = lax.dot_general(
            hidden[at, :], weights[1, cols, :], (((1,), (1,)), ((), ())),
            preferred_element_type=jnp.float32,
        )
        dest[:, cols] = value.astype(jnp.bfloat16)

    def exchange(i):
        cols = pl.ds(pl.multiple_of(i * COLS, COLS), COLS)
        return pltpu.make_async_remote_copy(
            src_ref=give.at[:, cols], dst_ref=take.at[:, cols],
            send_sem=give_sem.at[i], recv_sem=take_sem.at[i],
            device_id={"mp": 1 - m}, device_id_type=MESH,
        )

    def other_half(i, carry):
        down((1 - m) * half, give, i)
        exchange(i).start()
        return carry

    def own_half(i, carry):
        down(m * half, own, i)
        return carry

    steps = width // COLS
    lax.fori_loop(0, steps, other_half, 0)
    lax.fori_loop(0, steps, own_half, 0)
    for i in range(steps):
        exchange(i).wait_recv()

    def second_norm(i, carry):
        at = pl.ds(pl.multiple_of(i * rows, rows), rows)
        whole = pl.ds(pl.multiple_of(m * half + i * rows, rows), rows)
        mixed = own[at, :].astype(jnp.float32) + take[at, :].astype(jnp.float32)
        value = xs[whole, :].astype(jnp.float32) + mixed
        normed[at, :] = layer_norm(value, gains[1:2, :]).astype(jnp.bfloat16)
        return carry

    lax.fori_loop(0, half // rows, second_norm, 0)
    local[3].wait()
    values = jnp.dot(
        normed[0:half, :], neck[...], preferred_element_type=jnp.float32
    ).astype(jnp.bfloat16)
    tile_size = side * side
    for slot in range(part):
        value = values[slot * tile_size : (slot + 1) * tile_size]
        top = table[0, 0, z * slots + m * part + slot]
        swapped = jnp.concatenate([value[tile_size // 2 :], value[: tile_size // 2]], axis=0)
        flag = jnp.bitwise_and(jnp.maximum(top, 0), side - 1) == side // 2
        value = jnp.where(flag, swapped.astype(jnp.float32), value.astype(jnp.float32)).astype(jnp.bfloat16)
        for row in range(side):
            at = slot * run + (row // enc) * side
            deal[row % enc, at : at + side, :] = value[row * side : (row + 1) * side]

    def deal_copy(off):
        target = (z + off) % enc
        return pltpu.make_async_remote_copy(
            src_ref=deal.at[target], dst_ref=dealt.at[z],
            send_sem=deal_send.at[off], recv_sem=deal_recv.at[off],
            device_id={"enc": target}, device_id_type=MESH,
        )

    for off in range(1, enc):
        deal_copy(off).start()
    dealt[z] = deal[z]
    local[4].wait()
    for off in range(1, enc):
        deal_copy(off).wait_recv()
    channels = deal.shape[2]
    numer = jnp.dot(
        spread[...], dealt[...].reshape(lanes, channels), preferred_element_type=jnp.float32
    )
    part_sum[...] = numer.astype(jnp.bfloat16)

    def pair(src, dst, which):
        return pltpu.make_async_remote_copy(
            src_ref=src, dst_ref=dst, send_sem=pair_send.at[which], recv_sem=pair_recv.at[which],
            device_id={"mp": 1 - m}, device_id_type=MESH,
        )

    swap_sum = pair(part_sum, other_sum, 0)
    swap_sum.start()
    swap_sum.wait_recv()
    numer = part_sum[...].astype(jnp.float32) + other_sum[...].astype(jnp.float32)
    whole = numer / denom[...]
    merged[...] = whole.astype(jnp.bfloat16)

    def halo_copy(which):
        return pltpu.make_async_remote_copy(
            src_ref=merged, dst_ref=halo.at[which],
            send_sem=halo_send.at[which], recv_sem=halo_recv.at[which],
            device_id={"enc": (below_z, above_z)[which]}, device_id_type=MESH,
        )

    halo_copy(0).start()
    halo_copy(1).start()
    cube = whole.reshape(spread_rows, band, channels)
    blank = jnp.zeros((edge.shape[1] - spread_rows, channels), jnp.float32)
    edge[0] = jnp.concatenate([cube[:, 0, :], blank], axis=0).astype(jnp.bfloat16)
    edge[1] = jnp.concatenate([cube[:, band - 1, :], blank], axis=0).astype(jnp.bfloat16)

    def edge_copy(which, level):
        target = {"dec": (x - 1, x + 1)[which]}
        if level:
            target["enc"] = (below_z, above_z)[level - 1]
        return pltpu.make_async_remote_copy(
            src_ref=edge.at[which], dst_ref=edges_in.at[1 - which, level],
            send_sem=edge_send.at[which, level], recv_sem=edge_recv.at[1 - which, level],
            device_id=target, device_id_type=MESH,
        )

    def every_edge(which, act):
        @pl.when((x > 0) if which == 0 else (x < dec - 1))
        def _():
            for level in range(3):
                act(edge_copy(which, level))

    every_edge(0, lambda c: c.start())
    every_edge(1, lambda c: c.start())

    kinds = conv_w.shape[3]

    def products(source, row_off):
        return [
            jnp.dot(source, conv_w[row_off, b], preferred_element_type=jnp.float32) for b in range(3)
        ]

    spot = lax.broadcasted_iota(jnp.int32, (spread_rows, band, kinds), 0).reshape(places, kinds)
    spot_col = lax.broadcasted_iota(jnp.int32, (spread_rows, band, kinds), 1).reshape(places, kinds)
    center = products(merged[...], 1)

    def moved_down(value, step, index):
        shifted_value = jnp.where(index == 0, 0.0, pltpu.roll(value, step, 0))
        return jnp.where(z == 0, shifted_value, value)

    def moved_up(value, step, index):
        size = value.shape[0]
        shifted_value = jnp.where(index == spread_rows - 1, 0.0, pltpu.roll(value, size - step, 0))
        return jnp.where(z == enc - 1, shifted_value, value)

    halo_copy(0).wait_recv()
    upper = products(halo[0], 0)
    halo_copy(1).wait_recv()
    lower = products(halo[1], 2)
    for which in range(2):
        every_edge(1 - which, lambda c: c.wait_send())

    @pl.when(x < dec - 1)
    def _():
        for level in range(3):
            edge_copy(0, level).wait_recv()

    @pl.when(x > 0)
    def _():
        for level in range(3):
            edge_copy(1, level).wait_recv()

    sums = [
        center[b] + moved_down(upper[b], band, spot) + moved_up(lower[b], band, spot) for b in range(3)
    ]
    index = lax.broadcasted_iota(jnp.int32, (edge.shape[1], kinds), 0)

    def edge_sum(which, b):
        levels = [
            jnp.dot(edges_in[which, level], conv_w[a, b], preferred_element_type=jnp.float32)
            for level, a in ((0, 1), (1, 0), (2, 2))
        ]
        value = levels[0] + moved_down(levels[1], 1, index) + moved_up(levels[2], 1, index)
        value = value[:spread_rows].reshape(spread_rows, 1, kinds)
        return jnp.broadcast_to(value, (spread_rows, band, kinds)).reshape(places, kinds)

    before = jnp.where(spot_col == 0, edge_sum(0, 0), pltpu.roll(sums[0], 1, 0))
    after = jnp.where(spot_col == band - 1, edge_sum(1, 2), pltpu.roll(sums[2], places - 1, 0))
    activ = jnp.maximum(sums[1] + before + after + conv_bias[...], 0.0).astype(jnp.bfloat16)
    part_logits[...] = lax.dot_general(
        cls_t[...], activ, (((1,), (1,)), ((), ())), preferred_element_type=jnp.float32
    )
    swap_logits = pair(part_logits, other_logits, 1)
    swap_logits.start()
    swap_logits.wait_recv()
    classes = out.shape[1]
    square = (classes, classes)
    same = lax.broadcasted_iota(jnp.int32, square, 0) == lax.broadcasted_iota(jnp.int32, square, 1)
    bias = jnp.sum(jnp.where(same, cls_bias[...], 0.0), axis=1, keepdims=True)
    logits = part_logits[...] + other_logits[...] + bias
    wanted = jnp.concatenate([labels[k] for k in range(spread_rows)], axis=1)
    ids = lax.broadcasted_iota(jnp.int32, (classes, places), 0)
    picked = jnp.sum(jnp.where(ids == wanted, logits, 0.0), axis=0, keepdims=True)
    nll = jnp.log(jnp.sum(jnp.exp(logits), axis=0, keepdims=True)) - picked
    for k in range(spread_rows):
        out_nll[k] = nll[:, k * band : (k + 1) * band]
        out[k] = logits[:, k * band : (k + 1) * band].reshape(classes, 1, band)

    swap_sum.wait_send()
    swap_logits.wait_send()
    halo_copy(0).wait_send()
    halo_copy(1).wait_send()
    for off in range(1, enc):
        deal_copy(off).wait_send()
    finish_sends(0)
    finish_sends(1)
    for i in range(steps):
        exchange(i).wait_send()


def body(
    tokens,
    gain_pre,
    w_up,
    w_down,
    gain_post,
    w_neck,
    conv_weight,
    conv_bias,
    cls_weight,
    cls_bias,
    tile_table,
    labels,
):
    sizes = tuple(lax.axis_size(name) for name in ("groups", "enc", "dec"))
    enc = sizes[1]
    blk, ff = w_up.shape
    width = tokens.shape[-1]
    flat = tokens.reshape(-1, width)
    total = flat.shape[0]
    half = total // 2
    rows_local, _, band = labels.shape
    places = rows_local * band
    channels = w_neck.shape[1]
    classes = cls_weight.shape[1]
    dealt_rows = half // enc
    edge_rows = -(-rows_local // 16) * 16
    bf16, f32 = jnp.bfloat16, jnp.float32
    vmem = pl.BlockSpec(memory_space=pltpu.VMEM)
    anywhere = pl.BlockSpec(memory_space=pl.ANY)
    dma = pltpu.SemaphoreType.DMA
    logits, nll = pl.pallas_call(
        functools.partial(strip_kernel, sizes, rows_local),
        out_shape=(
            jax.ShapeDtypeStruct((rows_local, classes, 1, band), f32),
            jax.ShapeDtypeStruct(labels.shape, f32),
        ),
        in_specs=[anywhere, vmem, anywhere, anywhere, vmem, anywhere, anywhere, vmem, vmem,
                  pl.BlockSpec(memory_space=pltpu.SMEM), vmem, vmem],
        out_specs=(vmem, vmem),
        scratch_shapes=[
            pltpu.VMEM((2, width), f32),
            pltpu.VMEM((2, width, ff), bf16),
            pltpu.VMEM((total, width), bf16),
            pltpu.VMEM((total, width), bf16),
            pltpu.VMEM((total, ff), bf16),
            pltpu.VMEM((half, width), bf16),
            pltpu.VMEM((half, width), bf16),
            pltpu.VMEM((half, width), bf16),
            pltpu.VMEM(w_neck.shape, bf16),
            pltpu.VMEM(conv_weight.shape, bf16),
            pltpu.VMEM((enc, dealt_rows, channels), bf16),
            pltpu.VMEM((enc, dealt_rows, channels), bf16),
            pltpu.VMEM((places, half), bf16),
            pltpu.VMEM((places, 1), f32),
            pltpu.VMEM((places, channels), bf16),
            pltpu.VMEM((places, channels), bf16),
            pltpu.VMEM((places, channels), bf16),
            pltpu.VMEM((2, places, channels), bf16),
            pltpu.VMEM((2, edge_rows, channels), bf16),
            pltpu.VMEM((2, 3, edge_rows, channels), bf16),
            pltpu.VMEM((classes, places), f32),
            pltpu.VMEM((classes, places), f32),
            dma((5,)),
            dma((2, enc, 4)),
            dma((2, enc, 6)),
            dma((width // COLS,)),
            dma((width // COLS,)),
            dma((enc,)),
            dma((enc,)),
            dma((2,)),
            dma((2,)),
            dma((2,)),
            dma((2,)),
            dma((2, 3)),
            dma((2, 3)),
        ],
        compiler_params=pltpu.CompilerParams(
            collective_id=0, has_side_effects=True, vmem_limit_bytes=60 * 1024 * 1024
        ),
    )(
        flat, gain_pre.reshape(-1, 128), w_up, w_down.T, gain_post.reshape(-1, 128), w_neck,
        conv_weight, conv_bias.reshape(1, -1), cls_weight.T, jnp.swapaxes(tile_table, 1, 2),
        cls_bias.reshape(1, -1), labels,
    )
    logits = jnp.transpose(logits, (0, 2, 3, 1))
    return (logits, nll)


def solution(mesh):
    in_specs = (
        P(("groups", "dec"), "enc", None, None, None),
        P(),
        P("enc", "mp"),
        P("mp", "enc"),
        P(),
        P(),
        P(None, None, None, "mp"),
        P("mp"),
        P("mp", None),
        P(),
        P(("groups", "dec"), None, None),
        P(None, "enc", ("groups", "dec")),
    )
    out_specs = (P(None, "enc", ("groups", "dec"), None), P(None, "enc", ("groups", "dec")))
    return jax.shard_map(body, mesh=mesh, in_specs=in_specs, out_specs=out_specs, check_vma=False)
```

```python
import functools

import jax
import jax.numpy as jnp
from jax import lax
from jax.experimental import pallas as pl
from jax.experimental.pallas import tpu as pltpu
from jax.sharding import PartitionSpec as P

TS = 16


norm_eps = 1e-05
blend_sigma = 4.0


def layer_norm(values, scale_vec):
    row_mean = jnp.mean(values, axis=-1, keepdims=True)
    centered = values - row_mean
    row_var = jnp.mean(centered * centered, axis=-1, keepdims=True)
    return centered * lax.rsqrt(row_var + norm_eps) * scale_vec


MESH = pl.DeviceIdType.MESH
COLS = 256


def strip_kernel(
    sizes, sizes_rows, tok, gain_pre, w_up, w_down_t, gain_post, w_neck, conv_hbm, conv_bias, cls_t, table,
    cls_bias, labels, out, out_nll,
    gains, weights, xs, normed, hidden, give, take, own, neck,
    conv_w, deal, dealt, spread, denom, part_sum, other_sum, merged, halo, edge, edges_in,
    part_logits, other_logits,
    local_sem, recv_sem, send_sem, give_sem, take_sem,
    deal_send, deal_recv, pair_send, pair_recv, halo_send, halo_recv, edge_send, edge_recv,
):
    groups, enc, dec = sizes
    y, z = lax.axis_index("groups"), lax.axis_index("enc")
    x, m = lax.axis_index("dec"), lax.axis_index("mp")
    blk, ff = w_up.shape
    total, width = xs.shape
    spread_rows = sizes_rows
    half = total // 2
    split = groups % 2 == 0 and dec % 2 == 0 and blk % 64 == 0
    parts = 4 if split else 1
    piece = blk // parts
    ox, oy = x + 1 - 2 * (x % 2), y + 1 - 2 * (y % 2)
    mine = (y % 2) * 2 + x % 2 if split else 0
    of_x = (y % 2) * 2 + 1 - x % 2
    of_y = (1 - y % 2) * 2 + x % 2
    diagonal = (1 - y % 2) * 2 + 1 - x % 2

    def region(mat, block, quarter):
        start = pl.multiple_of(block * blk + quarter * piece, 16)
        return weights.at[mat, pl.ds(start, piece)]

    def copy(mat, block, quarter, kind, target, sent, own_src=False):
        dst = region(mat, block, quarter)
        src = dst
        if own_src:
            start = pl.multiple_of(quarter * piece, 16)
            src = (w_up, w_down_t)[mat].at[pl.ds(start, piece)]
        return pltpu.make_async_remote_copy(
            src_ref=src, dst_ref=dst,
            send_sem=send_sem.at[mat, block, sent], recv_sem=recv_sem.at[mat, block, kind],
            device_id=target, device_id_type=MESH,
        )

    up_z, down_z = {"enc": z + 1}, {"enc": z - 1}
    to_x, to_y = {"dec": ox}, {"groups": oy}

    def own_sends(mat):
        right = copy(mat, z, mine, 0, up_z, 0, True)
        left = copy(mat, z, mine, 0, down_z, 1, True)
        if not split:
            return (right,), (left,)
        right_diagonal = copy(mat, z, diagonal, 3, up_z, 4, True)
        left_diagonal = copy(mat, z, diagonal, 3, down_z, 5, True)
        return (right, right_diagonal), (left, left_diagonal)

    def start_own(mat, first, last):
        right, left = own_sends(mat)
        right, left = right[first:last], left[first:last]

        @pl.when(z < enc - 1)
        def _():
            for item in right:
                item.start()

        @pl.when(z > 0)
        def _():
            for item in left:
                item.start()

    def z_step(mat, far):
        @pl.when(z - far >= 0)
        def _():
            block = z - far
            copy(mat, block, mine, 0, up_z, 0).wait_recv()

            @pl.when(z < enc - 1)
            def _():
                copy(mat, block, mine, 0, up_z, 0).start()

            if split:
                copy(mat, block, mine, 1, to_x, 2).start()
                copy(mat, block, mine, 2, to_y, 3).start()

        @pl.when(z + far < enc)
        def _():
            block = z + far
            copy(mat, block, mine, 0, down_z, 1).wait_recv()

            @pl.when(z > 0)
            def _():
                copy(mat, block, mine, 0, down_z, 1).start()

            if split:
                copy(mat, block, mine, 1, to_x, 2).start()
                copy(mat, block, mine, 2, to_y, 3).start()

    def each_block(far, fn):
        @pl.when(z - far >= 0)
        def _():
            fn(z - far)

        @pl.when(z + far < enc)
        def _():
            fn(z + far)

    def plane_step(mat, far):
        if not split:
            return

        def one(block):
            by_y = (block + mat) % 2 == 0
            copy(mat, block, of_x, 1, to_x, 2).wait_recv()

            if far > 1:
                @pl.when(by_y)
                def _():
                    copy(mat, block, of_x, 3, to_y, 4).start()

            copy(mat, block, of_y, 2, to_y, 3).wait_recv()

            if far > 1:
                @pl.when(jnp.logical_not(by_y))
                def _():
                    copy(mat, block, of_y, 3, to_x, 4).start()

        each_block(far, one)

    def diagonal_step(mat, far):
        if split:
            each_block(far, lambda block: copy(mat, block, diagonal, 3, to_x, 4).wait_recv())

    def finish_sends(mat):
        right, left = own_sends(mat)

        @pl.when(z < enc - 1)
        def _():
            for item in right:
                item.wait_send()

        @pl.when(z > 0)
        def _():
            for item in left:
                item.wait_send()

        for far in range(1, enc):
            @pl.when((z - far >= 0) & (z < enc - 1))
            def _(far=far):
                copy(mat, z - far, mine, 0, up_z, 0).wait_send()

            @pl.when((z + far < enc) & (z > 0))
            def _(far=far):
                copy(mat, z + far, mine, 0, down_z, 1).wait_send()

            if split:
                def one(block, far=far):
                    copy(mat, block, mine, 1, to_x, 2).wait_send()
                    copy(mat, block, mine, 2, to_y, 3).wait_send()
                    if far > 1:
                        copy(mat, block, of_x, 3, to_x, 4).wait_send()

                each_block(far, one)

    start_of = pl.multiple_of(z * blk, 16)
    local = [
        pltpu.make_async_copy(tok, xs, local_sem.at[0]),
        pltpu.make_async_copy(w_up, weights.at[0, pl.ds(start_of, blk)], local_sem.at[1]),
        pltpu.make_async_copy(w_down_t, weights.at[1, pl.ds(start_of, blk)], local_sem.at[2]),
        pltpu.make_async_copy(w_neck, neck, local_sem.at[3]),
        pltpu.make_async_copy(conv_hbm, conv_w, local_sem.at[4]),
    ]
    for item in local:
        item.start()

    edges_in[...] = jnp.zeros_like(edges_in)
    above_z, below_z = (z + enc - 1) % enc, (z + 1) % enc
    barrier = pltpu.get_barrier_semaphore()

    def greet(**target):
        pl.semaphore_signal(barrier, inc=1, device_id=target, device_id_type=MESH)

    for off in range(1, enc):
        greet(enc=(z + off) % enc)
    greet(mp=1 - m)
    if split:
        greet(groups=oy)

    def greet_side(side_x):
        greet(dec=side_x)
        greet(dec=side_x, enc=above_z)
        greet(dec=side_x, enc=below_z)

    @pl.when(x > 0)
    def _():
        greet_side(x - 1)

    @pl.when(x < dec - 1)
    def _():
        greet_side(x + 1)

    sides = (x + dec - 1) // dec + 1 - (x + 1) // dec
    pl.semaphore_wait(barrier, enc + (1 if split else 0) + 3 * sides)

    start_own(0, 0, 1)
    local[0].wait()
    rows = 32

    def wide(ref):
        return jnp.concatenate([ref[i : i + 1, :] for i in range(ref.shape[0])], axis=1)

    gains[0:1, :] = wide(gain_pre)
    gains[1:2, :] = wide(gain_post)

    def first_norm(i, carry):
        at = pl.ds(pl.multiple_of(i * rows, rows), rows)
        normed[at, :] = layer_norm(xs[at, :].astype(jnp.float32), gains[0:1, :]).astype(jnp.bfloat16)
        return carry

    norm_steps = total // rows
    lax.fori_loop(0, norm_steps // 2, first_norm, 0)
    z_step(0, 1)
    lax.fori_loop(norm_steps // 2, norm_steps, first_norm, 0)
    for far in range(2, enc - 1):
        z_step(0, far)
    start_own(0, 1, 2)
    start_own(1, 0, 1)

    side = TS
    slots = total // (side * side)
    part = slots // 2
    row_groups = side // enc
    run = row_groups * side
    band = denom.shape[0] // spread_rows
    places = spread_rows * band
    lanes = enc * part * run
    lane = lax.broadcasted_iota(jnp.int32, (1, lanes), 1)
    strip_row = lax.broadcasted_iota(jnp.int32, (spread_rows, band, lanes), 0) * enc + z
    strip_row = strip_row.reshape(places, lanes)
    band_col = lax.broadcasted_iota(jnp.int32, (spread_rows, band, lanes), 1).reshape(places, lanes)

    def spread_of(owner):
        top = jnp.zeros((1, lanes), jnp.int32)
        left = jnp.zeros((1, lanes), jnp.int32)
        group = jnp.zeros((1, lanes), jnp.int32)
        col = lane
        for unit in range(enc * part):
            entry = (unit // part) * slots + owner * part + unit % part
            inside = lane >= unit * run
            top = jnp.where(inside, table[0, 0, entry], top)
            left = jnp.where(inside, table[0, 1, entry], left)
            for g in range(row_groups):
                begin = lane >= unit * run + g * side
                group = jnp.where(begin, g, group)
                col = jnp.where(begin, lane - (unit * run + g * side), col)
        tile_row = jnp.bitwise_and(group * enc + z - top, side - 1)
        middle = (side - 1) / 2.0
        dr = tile_row.astype(jnp.float32) - middle
        dc = col.astype(jnp.float32) - middle
        weight = jnp.exp(-(dr * dr + dc * dc) / (2.0 * blend_sigma * blend_sigma))
        weight = weight.astype(jnp.bfloat16).astype(jnp.float32)
        weight = jnp.where(top >= 0, weight, 0.0)
        hit = (strip_row == top + tile_row) & (band_col == left + col)
        return jnp.where(hit, weight, 0.0)

    mine_spread = spread_of(m)
    spread[...] = mine_spread.astype(jnp.bfloat16)
    denom[...] = jnp.sum(mine_spread + spread_of(1 - m), axis=1, keepdims=True)

    far_all = range(1, enc)
    if enc > 2:
        z_step(0, enc - 1)
    for far in range(2, enc):
        plane_step(0, far)
    z_step(1, 1)
    plane_step(0, 1)
    for far in far_all:
        diagonal_step(0, far)
    local[1].wait()

    col_steps = ff // COLS
    units = col_steps * 2

    def up_unit(i, carry):
        at = pl.ds(pl.multiple_of((i % 2) * half, half), half)
        cols = pl.ds(pl.multiple_of((i // 2) * COLS, COLS), COLS)
        value = jnp.dot(normed[at, :], weights[0, :, cols], preferred_element_type=jnp.float32)
        value = 0.5 * value * (1.0 + lax.erf(value * 0.7071067811865476))
        hidden[at, cols] = value.astype(jnp.bfloat16)
        return carry

    edges = [0, units // 5, units // 2, units * 7 // 10, units]
    lax.fori_loop(edges[0], edges[1], up_unit, 0)
    for far in range(2, enc - 1):
        z_step(1, far)
    start_own(1, 1, 2)
    lax.fori_loop(edges[1], edges[2], up_unit, 0)
    if enc > 2:
        z_step(1, enc - 1)
    for far in range(2, enc - 1):
        plane_step(1, far)
    lax.fori_loop(edges[2], edges[3], up_unit, 0)
    if enc > 2:
        plane_step(1, enc - 1)
    lax.fori_loop(edges[3], edges[4], up_unit, 0)
    plane_step(1, 1)
    for far in far_all:
        diagonal_step(1, far)
    local[2].wait()

    def down(first, dest, i):
        at = pl.ds(pl.multiple_of(first, half), half)
        cols = pl.ds(pl.multiple_of(i * COLS, COLS), COLS)
        value = lax.dot_general(
            hidden[at, :], weights[1, cols, :], (((1,), (1,)), ((), ())),
            preferred_element_type=jnp.float32,
        )
        dest[:, cols] = value.astype(jnp.bfloat16)

    def exchange(i):
        cols = pl.ds(pl.multiple_of(i * COLS, COLS), COLS)
        return pltpu.make_async_remote_copy(
            src_ref=give.at[:, cols], dst_ref=take.at[:, cols],
            send_sem=give_sem.at[i], recv_sem=take_sem.at[i],
            device_id={"mp": 1 - m}, device_id_type=MESH,
        )

    def other_half(i, carry):
        down((1 - m) * half, give, i)
        exchange(i).start()
        return carry

    def own_half(i, carry):
        down(m * half, own, i)
        return carry

    steps = width // COLS
    lax.fori_loop(0, steps, other_half, 0)
    lax.fori_loop(0, steps, own_half, 0)
    for i in range(steps):
        exchange(i).wait_recv()

    def second_norm(i, carry):
        at = pl.ds(pl.multiple_of(i * rows, rows), rows)
        whole = pl.ds(pl.multiple_of(m * half + i * rows, rows), rows)
        mixed = own[at, :].astype(jnp.float32) + take[at, :].astype(jnp.float32)
        value = xs[whole, :].astype(jnp.float32) + mixed
        normed[at, :] = layer_norm(value, gains[1:2, :]).astype(jnp.bfloat16)
        return carry

    lax.fori_loop(0, half // rows, second_norm, 0)
    local[3].wait()
    values = jnp.dot(
        normed[0:half, :], neck[...], preferred_element_type=jnp.float32
    ).astype(jnp.bfloat16)
    tile_size = side * side
    for slot in range(part):
        value = values[slot * tile_size : (slot + 1) * tile_size]
        top = table[0, 0, z * slots + m * part + slot]
        swapped = jnp.concatenate([value[tile_size // 2 :], value[: tile_size // 2]], axis=0)
        flag = jnp.bitwise_and(jnp.maximum(top, 0), side - 1) == side // 2
        value = jnp.where(flag, swapped.astype(jnp.float32), value.astype(jnp.float32)).astype(jnp.bfloat16)
        for row in range(side):
            at = slot * run + (row // enc) * side
            deal[row % enc, at : at + side, :] = value[row * side : (row + 1) * side]

    def deal_copy(off):
        target = (z + off) % enc
        return pltpu.make_async_remote_copy(
            src_ref=deal.at[target], dst_ref=dealt.at[z],
            send_sem=deal_send.at[off], recv_sem=deal_recv.at[off],
            device_id={"enc": target}, device_id_type=MESH,
        )

    for off in range(1, enc):
        deal_copy(off).start()
    dealt[z] = deal[z]
    local[4].wait()
    for off in range(1, enc):
        deal_copy(off).wait_recv()
    channels = deal.shape[2]
    numer = jnp.dot(
        spread[...], dealt[...].reshape(lanes, channels), preferred_element_type=jnp.float32
    )
    part_sum[...] = numer.astype(jnp.bfloat16)

    def pair(src, dst, which):
        return pltpu.make_async_remote_copy(
            src_ref=src, dst_ref=dst, send_sem=pair_send.at[which], recv_sem=pair_recv.at[which],
            device_id={"mp": 1 - m}, device_id_type=MESH,
        )

    swap_sum = pair(part_sum, other_sum, 0)
    swap_sum.start()
    swap_sum.wait_recv()
    numer = part_sum[...].astype(jnp.float32) + other_sum[...].astype(jnp.float32)
    whole = numer / denom[...]
    merged[...] = whole.astype(jnp.bfloat16)

    def halo_copy(which):
        return pltpu.make_async_remote_copy(
            src_ref=merged, dst_ref=halo.at[which],
            send_sem=halo_send.at[which], recv_sem=halo_recv.at[which],
            device_id={"enc": (below_z, above_z)[which]}, device_id_type=MESH,
        )

    halo_copy(0).start()
    halo_copy(1).start()
    cube = whole.reshape(spread_rows, band, channels)
    blank = jnp.zeros((edge.shape[1] - spread_rows, channels), jnp.float32)
    edge[0] = jnp.concatenate([cube[:, 0, :], blank], axis=0).astype(jnp.bfloat16)
    edge[1] = jnp.concatenate([cube[:, band - 1, :], blank], axis=0).astype(jnp.bfloat16)

    def edge_copy(which, level):
        target = {"dec": (x - 1, x + 1)[which]}
        if level:
            target["enc"] = (below_z, above_z)[level - 1]
        return pltpu.make_async_remote_copy(
            src_ref=edge.at[which], dst_ref=edges_in.at[1 - which, level],
            send_sem=edge_send.at[which, level], recv_sem=edge_recv.at[1 - which, level],
            device_id=target, device_id_type=MESH,
        )

    def every_edge(which, act):
        @pl.when((x > 0) if which == 0 else (x < dec - 1))
        def _():
            for level in range(3):
                act(edge_copy(which, level))

    every_edge(0, lambda c: c.start())
    every_edge(1, lambda c: c.start())

    kinds = conv_w.shape[3]

    def products(source, row_off):
        return [
            jnp.dot(source, conv_w[row_off, b], preferred_element_type=jnp.float32) for b in range(3)
        ]

    spot = lax.broadcasted_iota(jnp.int32, (spread_rows, band, kinds), 0).reshape(places, kinds)
    spot_col = lax.broadcasted_iota(jnp.int32, (spread_rows, band, kinds), 1).reshape(places, kinds)
    center = products(merged[...], 1)

    def moved_down(value, step, index):
        shifted_value = jnp.where(index == 0, 0.0, pltpu.roll(value, step, 0))
        return jnp.where(z == 0, shifted_value, value)

    def moved_up(value, step, index):
        size = value.shape[0]
        shifted_value = jnp.where(index == spread_rows - 1, 0.0, pltpu.roll(value, size - step, 0))
        return jnp.where(z == enc - 1, shifted_value, value)

    halo_copy(0).wait_recv()
    upper = products(halo[0], 0)
    halo_copy(1).wait_recv()
    lower = products(halo[1], 2)
    for which in range(2):
        every_edge(1 - which, lambda c: c.wait_send())

    @pl.when(x < dec - 1)
    def _():
        for level in range(3):
            edge_copy(0, level).wait_recv()

    @pl.when(x > 0)
    def _():
        for level in range(3):
            edge_copy(1, level).wait_recv()

    sums = [
        center[b] + moved_down(upper[b], band, spot) + moved_up(lower[b], band, spot) for b in range(3)
    ]
    index = lax.broadcasted_iota(jnp.int32, (edge.shape[1], kinds), 0)

    def edge_sum(which, b):
        levels = [
            jnp.dot(edges_in[which, level], conv_w[a, b], preferred_element_type=jnp.float32)
            for level, a in ((0, 1), (1, 0), (2, 2))
        ]
        value = levels[0] + moved_down(levels[1], 1, index) + moved_up(levels[2], 1, index)
        value = value[:spread_rows].reshape(spread_rows, 1, kinds)
        return jnp.broadcast_to(value, (spread_rows, band, kinds)).reshape(places, kinds)

    before = jnp.where(spot_col == 0, edge_sum(0, 0), pltpu.roll(sums[0], 1, 0))
    after = jnp.where(spot_col == band - 1, edge_sum(1, 2), pltpu.roll(sums[2], places - 1, 0))
    activ = jnp.maximum(sums[1] + before + after + conv_bias[...], 0.0).astype(jnp.bfloat16)
    part_logits[...] = lax.dot_general(
        cls_t[...], activ, (((1,), (1,)), ((), ())), preferred_element_type=jnp.float32
    )
    swap_logits = pair(part_logits, other_logits, 1)
    swap_logits.start()
    swap_logits.wait_recv()
    classes = out.shape[1]
    square = (classes, classes)
    same = lax.broadcasted_iota(jnp.int32, square, 0) == lax.broadcasted_iota(jnp.int32, square, 1)
    bias = jnp.sum(jnp.where(same, cls_bias[...], 0.0), axis=1, keepdims=True)
    logits = part_logits[...] + other_logits[...] + bias
    wanted = jnp.concatenate([labels[k] for k in range(spread_rows)], axis=1)
    ids = lax.broadcasted_iota(jnp.int32, (classes, places), 0)
    picked = jnp.sum(jnp.where(ids == wanted, logits, 0.0), axis=0, keepdims=True)
    nll = jnp.log(jnp.sum(jnp.exp(logits), axis=0, keepdims=True)) - picked
    for k in range(spread_rows):
        out_nll[k] = nll[:, k * band : (k + 1) * band]
        out[k] = logits[:, k * band : (k + 1) * band].reshape(classes, 1, band)

    swap_sum.wait_send()
    swap_logits.wait_send()
    halo_copy(0).wait_send()
    halo_copy(1).wait_send()
    for off in range(1, enc):
        deal_copy(off).wait_send()
    finish_sends(0)
    finish_sends(1)
    for i in range(steps):
        exchange(i).wait_send()


def body(
    tokens,
    gain_pre,
    w_up,
    w_down,
    gain_post,
    w_neck,
    conv_weight,
    conv_bias,
    cls_weight,
    cls_bias,
    tile_table,
    labels,
):
    sizes = tuple(lax.axis_size(name) for name in ("groups", "enc", "dec"))
    enc = sizes[1]
    blk, ff = w_up.shape
    width = tokens.shape[-1]
    flat = tokens.reshape(-1, width)
    total = flat.shape[0]
    half = total // 2
    rows_local, _, band = labels.shape
    places = rows_local * band
    channels = w_neck.shape[1]
    classes = cls_weight.shape[1]
    dealt_rows = half // enc
    edge_rows = -(-rows_local // 16) * 16
    bf16, f32 = jnp.bfloat16, jnp.float32
    vmem = pl.BlockSpec(memory_space=pltpu.VMEM)
    anywhere = pl.BlockSpec(memory_space=pl.ANY)
    dma = pltpu.SemaphoreType.DMA
    logits, nll = pl.pallas_call(
        functools.partial(strip_kernel, sizes, rows_local),
        out_shape=(
            jax.ShapeDtypeStruct((rows_local, classes, 1, band), f32),
            jax.ShapeDtypeStruct(labels.shape, f32),
        ),
        in_specs=[anywhere, vmem, anywhere, anywhere, vmem, anywhere, anywhere, vmem, vmem,
                  pl.BlockSpec(memory_space=pltpu.SMEM), vmem, vmem],
        out_specs=(vmem, vmem),
        scratch_shapes=[
            pltpu.VMEM((2, width), f32),
            pltpu.VMEM((2, width, ff), bf16),
            pltpu.VMEM((total, width), bf16),
            pltpu.VMEM((total, width), bf16),
            pltpu.VMEM((total, ff), bf16),
            pltpu.VMEM((half, width), bf16),
            pltpu.VMEM((half, width), bf16),
            pltpu.VMEM((half, width), bf16),
            pltpu.VMEM(w_neck.shape, bf16),
            pltpu.VMEM(conv_weight.shape, bf16),
            pltpu.VMEM((enc, dealt_rows, channels), bf16),
            pltpu.VMEM((enc, dealt_rows, channels), bf16),
            pltpu.VMEM((places, half), bf16),
            pltpu.VMEM((places, 1), f32),
            pltpu.VMEM((places, channels), bf16),
            pltpu.VMEM((places, channels), bf16),
            pltpu.VMEM((places, channels), bf16),
            pltpu.VMEM((2, places, channels), bf16),
            pltpu.VMEM((2, edge_rows, channels), bf16),
            pltpu.VMEM((2, 3, edge_rows, channels), bf16),
            pltpu.VMEM((classes, places), f32),
            pltpu.VMEM((classes, places), f32),
            dma((5,)),
            dma((2, enc, 4)),
            dma((2, enc, 6)),
            dma((width // COLS,)),
            dma((width // COLS,)),
            dma((enc,)),
            dma((enc,)),
            dma((2,)),
            dma((2,)),
            dma((2,)),
            dma((2,)),
            dma((2, 3)),
            dma((2, 3)),
        ],
        compiler_params=pltpu.CompilerParams(
            collective_id=0, has_side_effects=True, vmem_limit_bytes=60 * 1024 * 1024
        ),
    )(
        flat, gain_pre.reshape(-1, 128), w_up, w_down.T, gain_post.reshape(-1, 128), w_neck,
        conv_weight, conv_bias.reshape(1, -1), cls_weight.T, jnp.swapaxes(tile_table, 1, 2),
        cls_bias.reshape(1, -1), labels,
    )
    logits = jnp.transpose(logits, (0, 2, 3, 1))
    return (logits, nll)


def solution(mesh):
    in_specs = (
        P(("groups", "dec"), "enc", None, None, None),
        P(),
        P("enc", "mp"),
        P("mp", "enc"),
        P(),
        P(),
        P(None, None, None, "mp"),
        P("mp"),
        P("mp", None),
        P(),
        P(("groups", "dec"), None, None),
        P(None, "enc", ("groups", "dec")),
    )
    out_specs = (P(None, "enc", ("groups", "dec"), None), P(None, "enc", ("groups", "dec")))
    return jax.shard_map(body, mesh=mesh, in_specs=in_specs, out_specs=out_specs, check_vma=False)
```

```python
import functools

import jax
import jax.numpy as jnp
from jax import lax
from jax.experimental import pallas as pl
from jax.experimental.pallas import tpu as pltpu
from jax.sharding import PartitionSpec as P

TS = 16


norm_eps = 1e-05
blend_sigma = 4.0


def layer_norm(values, scale_vec):
    row_mean = jnp.mean(values, axis=-1, keepdims=True)
    centered = values - row_mean
    row_var = jnp.mean(centered * centered, axis=-1, keepdims=True)
    return centered * lax.rsqrt(row_var + norm_eps) * scale_vec


MESH = pl.DeviceIdType.MESH
COLS = 256


def strip_kernel(
    sizes, sizes_rows, tok, gain_pre, w_up, w_down_t, gain_post, w_neck, conv_hbm, conv_bias, cls_t, table,
    cls_bias, labels, out, out_nll,
    gains, weights, xs, normed, hidden, give, take, own, neck,
    conv_w, deal, dealt, spread, denom, part_sum, other_sum, merged, halo, edge, edges_in,
    part_logits, other_logits,
    local_sem, recv_sem, send_sem, give_sem, take_sem,
    deal_send, deal_recv, pair_send, pair_recv, halo_send, halo_recv, edge_send, edge_recv,
):
    groups, enc, dec = sizes
    y, z = lax.axis_index("groups"), lax.axis_index("enc")
    x, m = lax.axis_index("dec"), lax.axis_index("mp")
    blk, ff = w_up.shape
    half_ff = ff // 2
    total, width = xs.shape
    spread_rows = sizes_rows
    half = total // 2
    split = groups % 2 == 0 and dec % 2 == 0 and blk % 64 == 0
    parts = 4 if split else 1
    piece = blk // parts
    ox, oy = x + 1 - 2 * (x % 2), y + 1 - 2 * (y % 2)
    mine = (y % 2) * 2 + x % 2 if split else 0
    of_x = (y % 2) * 2 + 1 - x % 2
    of_y = (1 - y % 2) * 2 + x % 2
    diagonal = (1 - y % 2) * 2 + 1 - x % 2

    def region(mat, block, quarter):
        start = pl.multiple_of(block * blk + quarter * piece, 16)
        return weights.at[mat, pl.ds(start, piece)]

    def copy(mat, block, quarter, kind, target, sent, own_src=False):
        dst = region(mat, block, quarter)
        src = dst
        if own_src:
            start = pl.multiple_of(quarter * piece, 16)
            src = (w_up, w_down_t)[mat // 2].at[
                pl.ds(start, piece), pl.ds((mat % 2) * half_ff, half_ff)
            ]
        return pltpu.make_async_remote_copy(
            src_ref=src, dst_ref=dst,
            send_sem=send_sem.at[mat, block, sent], recv_sem=recv_sem.at[mat, block, kind],
            device_id=target, device_id_type=MESH,
        )

    up_z, down_z = {"enc": z + 1}, {"enc": z - 1}
    to_x, to_y = {"dec": ox}, {"groups": oy}

    def own_sends(mat):
        right = copy(mat, z, mine, 0, up_z, 0, True)
        left = copy(mat, z, mine, 0, down_z, 1, True)
        if not split:
            return (right,), (left,)
        right_diagonal = copy(mat, z, diagonal, 3, up_z, 4, True)
        left_diagonal = copy(mat, z, diagonal, 3, down_z, 5, True)
        return (right, right_diagonal), (left, left_diagonal)

    def start_own(mat, first, last):
        right, left = own_sends(mat)
        right, left = right[first:last], left[first:last]

        @pl.when(z < enc - 1)
        def _():
            for item in right:
                item.start()

        @pl.when(z > 0)
        def _():
            for item in left:
                item.start()

    def z_step(mat, far):
        @pl.when(z - far >= 0)
        def _():
            block = z - far
            copy(mat, block, mine, 0, up_z, 0).wait_recv()

            @pl.when(z < enc - 1)
            def _():
                copy(mat, block, mine, 0, up_z, 0).start()

            if split:
                copy(mat, block, mine, 1, to_x, 2).start()
                copy(mat, block, mine, 2, to_y, 3).start()

        @pl.when(z + far < enc)
        def _():
            block = z + far
            copy(mat, block, mine, 0, down_z, 1).wait_recv()

            @pl.when(z > 0)
            def _():
                copy(mat, block, mine, 0, down_z, 1).start()

            if split:
                copy(mat, block, mine, 1, to_x, 2).start()
                copy(mat, block, mine, 2, to_y, 3).start()

    def each_block(far, fn):
        @pl.when(z - far >= 0)
        def _():
            fn(z - far)

        @pl.when(z + far < enc)
        def _():
            fn(z + far)

    def plane_step(mat, far):
        if not split:
            return

        def one(block):
            by_y = (block + mat) % 2 == 0
            copy(mat, block, of_x, 1, to_x, 2).wait_recv()

            if far > 1:
                @pl.when(by_y)
                def _():
                    copy(mat, block, of_x, 3, to_y, 4).start()

            copy(mat, block, of_y, 2, to_y, 3).wait_recv()

            if far > 1:
                @pl.when(jnp.logical_not(by_y))
                def _():
                    copy(mat, block, of_y, 3, to_x, 4).start()

        each_block(far, one)

    def diagonal_step(mat, far):
        if split:
            each_block(far, lambda block: copy(mat, block, diagonal, 3, to_x, 4).wait_recv())

    def finish_sends(mat):
        right, left = own_sends(mat)

        @pl.when(z < enc - 1)
        def _():
            for item in right:
                item.wait_send()

        @pl.when(z > 0)
        def _():
            for item in left:
                item.wait_send()

        for far in range(1, enc):
            @pl.when((z - far >= 0) & (z < enc - 1))
            def _(far=far):
                copy(mat, z - far, mine, 0, up_z, 0).wait_send()

            @pl.when((z + far < enc) & (z > 0))
            def _(far=far):
                copy(mat, z + far, mine, 0, down_z, 1).wait_send()

            if split:
                def one(block, far=far):
                    copy(mat, block, mine, 1, to_x, 2).wait_send()
                    copy(mat, block, mine, 2, to_y, 3).wait_send()
                    if far > 1:
                        copy(mat, block, of_x, 3, to_x, 4).wait_send()

                each_block(far, one)

    start_of = pl.multiple_of(z * blk, 16)
    local = [
        pltpu.make_async_copy(tok, xs, local_sem.at[0]),
        pltpu.make_async_copy(w_neck, neck, local_sem.at[3]),
        pltpu.make_async_copy(conv_hbm, conv_w, local_sem.at[4]),
    ] + [
        pltpu.make_async_copy(
            (w_up, w_down_t)[mat // 2].at[:, pl.ds((mat % 2) * half_ff, half_ff)],
            weights.at[mat, pl.ds(start_of, blk)],
            local_sem.at[(1, 2, 5, 6)[mat]],
        )
        for mat in range(4)
    ]
    for item in local:
        item.start()

    edges_in[...] = jnp.zeros_like(edges_in)
    above_z, below_z = (z + enc - 1) % enc, (z + 1) % enc
    barrier = pltpu.get_barrier_semaphore()

    def greet(**target):
        pl.semaphore_signal(barrier, inc=1, device_id=target, device_id_type=MESH)

    for off in range(1, enc):
        greet(enc=(z + off) % enc)
    greet(mp=1 - m)
    if split:
        greet(groups=oy)

    def greet_side(side_x):
        greet(dec=side_x)
        greet(dec=side_x, enc=above_z)
        greet(dec=side_x, enc=below_z)

    @pl.when(x > 0)
    def _():
        greet_side(x - 1)

    @pl.when(x < dec - 1)
    def _():
        greet_side(x + 1)

    sides = (x + dec - 1) // dec + 1 - (x + 1) // dec
    pl.semaphore_wait(barrier, enc + (1 if split else 0) + 3 * sides)

    start_own(0, 0, 1)
    local[0].wait()
    rows = 32

    def wide(ref):
        return jnp.concatenate([ref[i : i + 1, :] for i in range(ref.shape[0])], axis=1)

    gains[0:1, :] = wide(gain_pre)
    gains[1:2, :] = wide(gain_post)

    def first_norm(i, carry):
        at = pl.ds(pl.multiple_of(i * rows, rows), rows)
        normed[at, :] = layer_norm(xs[at, :].astype(jnp.float32), gains[0:1, :]).astype(jnp.bfloat16)
        return carry

    norm_steps = total // rows
    lax.fori_loop(0, norm_steps // 2, first_norm, 0)
    z_step(0, 1)
    lax.fori_loop(norm_steps // 2, norm_steps, first_norm, 0)
    for far in range(2, enc - 1):
        z_step(0, far)
    start_own(0, 1, 2)
    start_own(1, 0, 1)

    side = TS
    slots = total // (side * side)
    part = slots // 2
    row_groups = side // enc
    run = row_groups * side
    band = denom.shape[0] // spread_rows
    places = spread_rows * band
    lanes = enc * part * run
    lane = lax.broadcasted_iota(jnp.int32, (1, lanes), 1)
    strip_row = lax.broadcasted_iota(jnp.int32, (spread_rows, band, lanes), 0) * enc + z
    strip_row = strip_row.reshape(places, lanes)
    band_col = lax.broadcasted_iota(jnp.int32, (spread_rows, band, lanes), 1).reshape(places, lanes)

    def spread_of(owner):
        top = jnp.zeros((1, lanes), jnp.int32)
        left = jnp.zeros((1, lanes), jnp.int32)
        group = jnp.zeros((1, lanes), jnp.int32)
        col = lane
        for unit in range(enc * part):
            entry = (unit // part) * slots + owner * part + unit % part
            inside = lane >= unit * run
            top = jnp.where(inside, table[0, 0, entry], top)
            left = jnp.where(inside, table[0, 1, entry], left)
            for g in range(row_groups):
                begin = lane >= unit * run + g * side
                group = jnp.where(begin, g, group)
                col = jnp.where(begin, lane - (unit * run + g * side), col)
        tile_row = jnp.bitwise_and(group * enc + z - top, side - 1)
        middle = (side - 1) / 2.0
        dr = tile_row.astype(jnp.float32) - middle
        dc = col.astype(jnp.float32) - middle
        weight = jnp.exp(-(dr * dr + dc * dc) / (2.0 * blend_sigma * blend_sigma))
        weight = weight.astype(jnp.bfloat16).astype(jnp.float32)
        weight = jnp.where(top >= 0, weight, 0.0)
        hit = (strip_row == top + tile_row) & (band_col == left + col)
        return jnp.where(hit, weight, 0.0)

    mine_spread = spread_of(m)
    spread[...] = mine_spread.astype(jnp.bfloat16)
    denom[...] = jnp.sum(mine_spread + spread_of(1 - m), axis=1, keepdims=True)

    far_all = range(1, enc)
    row_chunk = total // 4

    def up_unit(mat):
        def unit(i, carry):
            at = pl.ds(pl.multiple_of(i * row_chunk, row_chunk), row_chunk)
            value = jnp.dot(normed[at, :], weights[mat], preferred_element_type=jnp.float32)
            value = 0.5 * value * (1.0 + lax.erf(value * 0.7071067811865476))
            hidden[at, mat * half_ff : (mat + 1) * half_ff] = value.astype(jnp.bfloat16)
            return carry

        return unit

    def rest_of(mat):
        if enc > 2:
            z_step(mat, enc - 1)
        for far in range(2, enc):
            plane_step(mat, far)
        if mat < 3:
            z_step(mat + 1, 1)
        plane_step(mat, 1)

    def early_of(mat):
        for far in range(2, enc - 1):
            z_step(mat, far)
        start_own(mat, 1, 2)
        if mat < 3:
            start_own(mat + 1, 0, 1)

    def last_of(mat):
        for far in far_all:
            diagonal_step(mat, far)
        local[3 + mat].wait()

    rest_of(0)
    early_of(1)
    last_of(0)
    lax.fori_loop(0, 2, up_unit(0), 0)
    rest_of(1)
    lax.fori_loop(2, 4, up_unit(0), 0)
    early_of(2)
    last_of(1)
    lax.fori_loop(0, 2, up_unit(1), 0)
    rest_of(2)
    early_of(3)
    lax.fori_loop(2, 4, up_unit(1), 0)
    last_of(2)
    rest_of(3)
    last_of(3)

    def down(first, dest, i):
        at = pl.ds(pl.multiple_of(first, half), half)
        cols = pl.ds(pl.multiple_of(i * COLS, COLS), COLS)
        value = sum(
            lax.dot_general(
                hidden[at, mat * half_ff : (mat + 1) * half_ff], weights[2 + mat, cols, :],
                (((1,), (1,)), ((), ())), preferred_element_type=jnp.float32,
            )
            for mat in range(2)
        )
        dest[:, cols] = value.astype(jnp.bfloat16)

    def exchange(i):
        cols = pl.ds(pl.multiple_of(i * COLS, COLS), COLS)
        return pltpu.make_async_remote_copy(
            src_ref=give.at[:, cols], dst_ref=take.at[:, cols],
            send_sem=give_sem.at[i], recv_sem=take_sem.at[i],
            device_id={"mp": 1 - m}, device_id_type=MESH,
        )

    def other_half(i, carry):
        down((1 - m) * half, give, i)
        exchange(i).start()
        return carry

    def own_half(i, carry):
        down(m * half, own, i)
        return carry

    steps = width // COLS
    lax.fori_loop(0, steps, other_half, 0)
    lax.fori_loop(0, steps, own_half, 0)
    for i in range(steps):
        exchange(i).wait_recv()

    def second_norm(i, carry):
        at = pl.ds(pl.multiple_of(i * rows, rows), rows)
        whole = pl.ds(pl.multiple_of(m * half + i * rows, rows), rows)
        mixed = own[at, :].astype(jnp.float32) + take[at, :].astype(jnp.float32)
        value = xs[whole, :].astype(jnp.float32) + mixed
        normed[at, :] = layer_norm(value, gains[1:2, :]).astype(jnp.bfloat16)
        return carry

    lax.fori_loop(0, half // rows, second_norm, 0)
    local[1].wait()
    values = jnp.dot(
        normed[0:half, :], neck[...], preferred_element_type=jnp.float32
    ).astype(jnp.bfloat16)
    tile_size = side * side
    for slot in range(part):
        value = values[slot * tile_size : (slot + 1) * tile_size]
        top = table[0, 0, z * slots + m * part + slot]
        swapped = jnp.concatenate([value[tile_size // 2 :], value[: tile_size // 2]], axis=0)
        flag = jnp.bitwise_and(jnp.maximum(top, 0), side - 1) == side // 2
        value = jnp.where(flag, swapped.astype(jnp.float32), value.astype(jnp.float32)).astype(jnp.bfloat16)
        for row in range(side):
            at = slot * run + (row // enc) * side
            deal[row % enc, at : at + side, :] = value[row * side : (row + 1) * side]

    def deal_copy(off):
        target = (z + off) % enc
        return pltpu.make_async_remote_copy(
            src_ref=deal.at[target], dst_ref=dealt.at[z],
            send_sem=deal_send.at[off], recv_sem=deal_recv.at[off],
            device_id={"enc": target}, device_id_type=MESH,
        )

    for off in range(1, enc):
        deal_copy(off).start()
    dealt[z] = deal[z]
    local[2].wait()
    for off in range(1, enc):
        deal_copy(off).wait_recv()
    channels = deal.shape[2]
    numer = jnp.dot(
        spread[...], dealt[...].reshape(lanes, channels), preferred_element_type=jnp.float32
    )
    part_sum[...] = numer.astype(jnp.bfloat16)

    def pair(src, dst, which):
        return pltpu.make_async_remote_copy(
            src_ref=src, dst_ref=dst, send_sem=pair_send.at[which], recv_sem=pair_recv.at[which],
            device_id={"mp": 1 - m}, device_id_type=MESH,
        )

    swap_sum = pair(part_sum, other_sum, 0)
    swap_sum.start()
    swap_sum.wait_recv()
    numer = part_sum[...].astype(jnp.float32) + other_sum[...].astype(jnp.float32)
    whole = numer / denom[...]
    merged[...] = whole.astype(jnp.bfloat16)

    def halo_copy(which):
        return pltpu.make_async_remote_copy(
            src_ref=merged, dst_ref=halo.at[which],
            send_sem=halo_send.at[which], recv_sem=halo_recv.at[which],
            device_id={"enc": (below_z, above_z)[which]}, device_id_type=MESH,
        )

    halo_copy(0).start()
    halo_copy(1).start()
    cube = whole.reshape(spread_rows, band, channels)
    blank = jnp.zeros((edge.shape[1] - spread_rows, channels), jnp.float32)
    edge[0] = jnp.concatenate([cube[:, 0, :], blank], axis=0).astype(jnp.bfloat16)
    edge[1] = jnp.concatenate([cube[:, band - 1, :], blank], axis=0).astype(jnp.bfloat16)

    def edge_copy(which, level):
        target = {"dec": (x - 1, x + 1)[which]}
        if level:
            target["enc"] = (below_z, above_z)[level - 1]
        return pltpu.make_async_remote_copy(
            src_ref=edge.at[which], dst_ref=edges_in.at[1 - which, level],
            send_sem=edge_send.at[which, level], recv_sem=edge_recv.at[1 - which, level],
            device_id=target, device_id_type=MESH,
        )

    def every_edge(which, act):
        @pl.when((x > 0) if which == 0 else (x < dec - 1))
        def _():
            for level in range(3):
                act(edge_copy(which, level))

    every_edge(0, lambda c: c.start())
    every_edge(1, lambda c: c.start())

    kinds = conv_w.shape[3]

    def products(source, row_off):
        return [
            jnp.dot(source, conv_w[row_off, b], preferred_element_type=jnp.float32) for b in range(3)
        ]

    spot = lax.broadcasted_iota(jnp.int32, (spread_rows, band, kinds), 0).reshape(places, kinds)
    spot_col = lax.broadcasted_iota(jnp.int32, (spread_rows, band, kinds), 1).reshape(places, kinds)
    center = products(merged[...], 1)

    def moved_down(value, step, index):
        shifted_value = jnp.where(index == 0, 0.0, pltpu.roll(value, step, 0))
        return jnp.where(z == 0, shifted_value, value)

    def moved_up(value, step, index):
        size = value.shape[0]
        shifted_value = jnp.where(index == spread_rows - 1, 0.0, pltpu.roll(value, size - step, 0))
        return jnp.where(z == enc - 1, shifted_value, value)

    halo_copy(0).wait_recv()
    upper = products(halo[0], 0)
    halo_copy(1).wait_recv()
    lower = products(halo[1], 2)
    for which in range(2):
        every_edge(1 - which, lambda c: c.wait_send())

    @pl.when(x < dec - 1)
    def _():
        for level in range(3):
            edge_copy(0, level).wait_recv()

    @pl.when(x > 0)
    def _():
        for level in range(3):
            edge_copy(1, level).wait_recv()

    sums = [
        center[b] + moved_down(upper[b], band, spot) + moved_up(lower[b], band, spot) for b in range(3)
    ]
    index = lax.broadcasted_iota(jnp.int32, (edge.shape[1], kinds), 0)

    def edge_sum(which, b):
        levels = [
            jnp.dot(edges_in[which, level], conv_w[a, b], preferred_element_type=jnp.float32)
            for level, a in ((0, 1), (1, 0), (2, 2))
        ]
        value = levels[0] + moved_down(levels[1], 1, index) + moved_up(levels[2], 1, index)
        value = value[:spread_rows].reshape(spread_rows, 1, kinds)
        return jnp.broadcast_to(value, (spread_rows, band, kinds)).reshape(places, kinds)

    before = jnp.where(spot_col == 0, edge_sum(0, 0), pltpu.roll(sums[0], 1, 0))
    after = jnp.where(spot_col == band - 1, edge_sum(1, 2), pltpu.roll(sums[2], places - 1, 0))
    activ = jnp.maximum(sums[1] + before + after + conv_bias[...], 0.0).astype(jnp.bfloat16)
    part_logits[...] = lax.dot_general(
        cls_t[...], activ, (((1,), (1,)), ((), ())), preferred_element_type=jnp.float32
    )
    swap_logits = pair(part_logits, other_logits, 1)
    swap_logits.start()
    swap_logits.wait_recv()
    classes = out.shape[1]
    square = (classes, classes)
    same = lax.broadcasted_iota(jnp.int32, square, 0) == lax.broadcasted_iota(jnp.int32, square, 1)
    bias = jnp.sum(jnp.where(same, cls_bias[...], 0.0), axis=1, keepdims=True)
    logits = part_logits[...] + other_logits[...] + bias
    wanted = jnp.concatenate([labels[k] for k in range(spread_rows)], axis=1)
    ids = lax.broadcasted_iota(jnp.int32, (classes, places), 0)
    picked = jnp.sum(jnp.where(ids == wanted, logits, 0.0), axis=0, keepdims=True)
    nll = jnp.log(jnp.sum(jnp.exp(logits), axis=0, keepdims=True)) - picked
    for k in range(spread_rows):
        out_nll[k] = nll[:, k * band : (k + 1) * band]
        out[k] = logits[:, k * band : (k + 1) * band].reshape(classes, 1, band)

    swap_sum.wait_send()
    swap_logits.wait_send()
    halo_copy(0).wait_send()
    halo_copy(1).wait_send()
    for off in range(1, enc):
        deal_copy(off).wait_send()
    for mat in range(4):
        finish_sends(mat)
    for i in range(steps):
        exchange(i).wait_send()


def body(
    tokens,
    gain_pre,
    w_up,
    w_down,
    gain_post,
    w_neck,
    conv_weight,
    conv_bias,
    cls_weight,
    cls_bias,
    tile_table,
    labels,
):
    sizes = tuple(lax.axis_size(name) for name in ("groups", "enc", "dec"))
    enc = sizes[1]
    blk, ff = w_up.shape
    width = tokens.shape[-1]
    flat = tokens.reshape(-1, width)
    total = flat.shape[0]
    half = total // 2
    rows_local, _, band = labels.shape
    places = rows_local * band
    channels = w_neck.shape[1]
    classes = cls_weight.shape[1]
    dealt_rows = half // enc
    edge_rows = -(-rows_local // 16) * 16
    bf16, f32 = jnp.bfloat16, jnp.float32
    vmem = pl.BlockSpec(memory_space=pltpu.VMEM)
    anywhere = pl.BlockSpec(memory_space=pl.ANY)
    dma = pltpu.SemaphoreType.DMA
    logits, nll = pl.pallas_call(
        functools.partial(strip_kernel, sizes, rows_local),
        out_shape=(
            jax.ShapeDtypeStruct((rows_local, classes, 1, band), f32),
            jax.ShapeDtypeStruct(labels.shape, f32),
        ),
        in_specs=[anywhere, vmem, anywhere, anywhere, vmem, anywhere, anywhere, vmem, vmem,
                  pl.BlockSpec(memory_space=pltpu.SMEM), vmem, vmem],
        out_specs=(vmem, vmem),
        scratch_shapes=[
            pltpu.VMEM((2, width), f32),
            pltpu.VMEM((4, width, ff // 2), bf16),
            pltpu.VMEM((total, width), bf16),
            pltpu.VMEM((total, width), bf16),
            pltpu.VMEM((total, ff), bf16),
            pltpu.VMEM((half, width), bf16),
            pltpu.VMEM((half, width), bf16),
            pltpu.VMEM((half, width), bf16),
            pltpu.VMEM(w_neck.shape, bf16),
            pltpu.VMEM(conv_weight.shape, bf16),
            pltpu.VMEM((enc, dealt_rows, channels), bf16),
            pltpu.VMEM((enc, dealt_rows, channels), bf16),
            pltpu.VMEM((places, half), bf16),
            pltpu.VMEM((places, 1), f32),
            pltpu.VMEM((places, channels), bf16),
            pltpu.VMEM((places, channels), bf16),
            pltpu.VMEM((places, channels), bf16),
            pltpu.VMEM((2, places, channels), bf16),
            pltpu.VMEM((2, edge_rows, channels), bf16),
            pltpu.VMEM((2, 3, edge_rows, channels), bf16),
            pltpu.VMEM((classes, places), f32),
            pltpu.VMEM((classes, places), f32),
            dma((7,)),
            dma((4, enc, 4)),
            dma((4, enc, 6)),
            dma((width // COLS,)),
            dma((width // COLS,)),
            dma((enc,)),
            dma((enc,)),
            dma((2,)),
            dma((2,)),
            dma((2,)),
            dma((2,)),
            dma((2, 3)),
            dma((2, 3)),
        ],
        compiler_params=pltpu.CompilerParams(
            collective_id=0, has_side_effects=True, vmem_limit_bytes=60 * 1024 * 1024
        ),
    )(
        flat, gain_pre.reshape(-1, 128), w_up, w_down.T, gain_post.reshape(-1, 128), w_neck,
        conv_weight, conv_bias.reshape(1, -1), cls_weight.T, jnp.swapaxes(tile_table, 1, 2),
        cls_bias.reshape(1, -1), labels,
    )
    logits = jnp.transpose(logits, (0, 2, 3, 1))
    return (logits, nll)


def solution(mesh):
    in_specs = (
        P(("groups", "dec"), "enc", None, None, None),
        P(),
        P("enc", "mp"),
        P("mp", "enc"),
        P(),
        P(),
        P(None, None, None, "mp"),
        P("mp"),
        P("mp", None),
        P(),
        P(("groups", "dec"), None, None),
        P(None, "enc", ("groups", "dec")),
    )
    out_specs = (P(None, "enc", ("groups", "dec"), None), P(None, "enc", ("groups", "dec")))
    return jax.shard_map(body, mesh=mesh, in_specs=in_specs, out_specs=out_specs, check_vma=False)
```

```python
import functools

import jax
import jax.numpy as jnp
from jax import lax
from jax.experimental import pallas as pl
from jax.experimental.pallas import tpu as pltpu
from jax.sharding import PartitionSpec as P

TS = 16


norm_eps = 1e-05
blend_sigma = 4.0


def layer_norm(values, scale_vec):
    row_mean = jnp.mean(values, axis=-1, keepdims=True)
    centered = values - row_mean
    row_var = jnp.mean(centered * centered, axis=-1, keepdims=True)
    return centered * lax.rsqrt(row_var + norm_eps) * scale_vec


MESH = pl.DeviceIdType.MESH
COLS = 256


def strip_kernel(
    sizes, sizes_rows, tok, gain_pre, w_up, w_down_t, gain_post, w_neck, conv_hbm, conv_bias, cls_t, table,
    cls_bias, labels, out, out_nll,
    gains, weights, xs, normed, hidden, give, take, neck,
    conv_w, deal, dealt, spread, denom, part_sum, other_sum, merged, halo, edge, edges_in,
    part_logits, other_logits,
    local_sem, recv_sem, send_sem, give_sem, take_sem,
    deal_send, deal_recv, pair_send, pair_recv, halo_send, halo_recv, edge_send, edge_recv,
):
    groups, enc, dec = sizes
    y, z = lax.axis_index("groups"), lax.axis_index("enc")
    x, m = lax.axis_index("dec"), lax.axis_index("mp")
    blk, ff = w_up.shape
    total, width = xs.shape
    spread_rows = sizes_rows
    half = total // 2
    split = groups % 2 == 0 and dec % 2 == 0 and blk % 64 == 0
    parts = 4 if split else 1
    piece = blk // parts
    ox, oy = x + 1 - 2 * (x % 2), y + 1 - 2 * (y % 2)
    mine = (y % 2) * 2 + x % 2 if split else 0
    of_x = (y % 2) * 2 + 1 - x % 2
    of_y = (1 - y % 2) * 2 + x % 2
    diagonal = (1 - y % 2) * 2 + 1 - x % 2

    def region(mat, block, quarter):
        start = pl.multiple_of(block * blk + quarter * piece, 16)
        return weights.at[mat, pl.ds(start, piece)]

    def copy(mat, block, quarter, kind, target, sent, own_src=False):
        dst = region(mat, block, quarter)
        src = dst
        if own_src:
            start = pl.multiple_of(quarter * piece, 16)
            src = (w_up, w_down_t)[mat].at[pl.ds(start, piece)]
        return pltpu.make_async_remote_copy(
            src_ref=src, dst_ref=dst,
            send_sem=send_sem.at[mat, block, sent], recv_sem=recv_sem.at[mat, block, kind],
            device_id=target, device_id_type=MESH,
        )

    up_z, down_z = {"enc": z + 1}, {"enc": z - 1}
    to_x, to_y = {"dec": ox}, {"groups": oy}

    def own_sends(mat):
        right = copy(mat, z, mine, 0, up_z, 0, True)
        left = copy(mat, z, mine, 0, down_z, 1, True)
        if not split:
            return (right,), (left,)
        right_diagonal = copy(mat, z, diagonal, 3, up_z, 4, True)
        left_diagonal = copy(mat, z, diagonal, 3, down_z, 5, True)
        return (right, right_diagonal), (left, left_diagonal)

    def start_own(mat, first, last):
        right, left = own_sends(mat)
        right, left = right[first:last], left[first:last]

        @pl.when(z < enc - 1)
        def _():
            for item in right:
                item.start()

        @pl.when(z > 0)
        def _():
            for item in left:
                item.start()

    def z_step(mat, far):
        @pl.when(z - far >= 0)
        def _():
            block = z - far
            copy(mat, block, mine, 0, up_z, 0).wait_recv()

            @pl.when(z < enc - 1)
            def _():
                copy(mat, block, mine, 0, up_z, 0).start()

            if split:
                copy(mat, block, mine, 1, to_x, 2).start()
                copy(mat, block, mine, 2, to_y, 3).start()

        @pl.when(z + far < enc)
        def _():
            block = z + far
            copy(mat, block, mine, 0, down_z, 1).wait_recv()

            @pl.when(z > 0)
            def _():
                copy(mat, block, mine, 0, down_z, 1).start()

            if split:
                copy(mat, block, mine, 1, to_x, 2).start()
                copy(mat, block, mine, 2, to_y, 3).start()

    def each_block(far, fn):
        @pl.when(z - far >= 0)
        def _():
            fn(z - far)

        @pl.when(z + far < enc)
        def _():
            fn(z + far)

    def plane_step(mat, far):
        if not split:
            return

        def one(block):
            by_y = (block + mat) % 2 == 0
            copy(mat, block, of_x, 1, to_x, 2).wait_recv()

            if far > 1:
                @pl.when(by_y)
                def _():
                    copy(mat, block, of_x, 3, to_y, 4).start()

            copy(mat, block, of_y, 2, to_y, 3).wait_recv()

            if far > 1:
                @pl.when(jnp.logical_not(by_y))
                def _():
                    copy(mat, block, of_y, 3, to_x, 4).start()

        each_block(far, one)

    def diagonal_step(mat, far):
        if split:
            each_block(far, lambda block: copy(mat, block, diagonal, 3, to_x, 4).wait_recv())

    def finish_sends(mat):
        right, left = own_sends(mat)

        @pl.when(z < enc - 1)
        def _():
            for item in right:
                item.wait_send()

        @pl.when(z > 0)
        def _():
            for item in left:
                item.wait_send()

        for far in range(1, enc):
            @pl.when((z - far >= 0) & (z < enc - 1))
            def _(far=far):
                copy(mat, z - far, mine, 0, up_z, 0).wait_send()

            @pl.when((z + far < enc) & (z > 0))
            def _(far=far):
                copy(mat, z + far, mine, 0, down_z, 1).wait_send()

            if split:
                def one(block, far=far):
                    copy(mat, block, mine, 1, to_x, 2).wait_send()
                    copy(mat, block, mine, 2, to_y, 3).wait_send()
                    if far > 1:
                        copy(mat, block, of_x, 3, to_x, 4).wait_send()

                each_block(far, one)

    start_of = pl.multiple_of(z * blk, 16)
    local = [
        pltpu.make_async_copy(tok, xs, local_sem.at[0]),
        pltpu.make_async_copy(w_up, weights.at[0, pl.ds(start_of, blk)], local_sem.at[1]),
        pltpu.make_async_copy(w_down_t, weights.at[1, pl.ds(start_of, blk)], local_sem.at[2]),
        pltpu.make_async_copy(w_neck, neck, local_sem.at[3]),
        pltpu.make_async_copy(conv_hbm, conv_w, local_sem.at[4]),
    ]
    for item in local:
        item.start()

    edges_in[...] = jnp.zeros_like(edges_in)
    above_z, below_z = (z + enc - 1) % enc, (z + 1) % enc
    barrier = pltpu.get_barrier_semaphore()

    def greet(**target):
        pl.semaphore_signal(barrier, inc=1, device_id=target, device_id_type=MESH)

    for off in range(1, enc):
        greet(enc=(z + off) % enc)
    greet(mp=1 - m)
    if split:
        greet(groups=oy)

    def greet_side(side_x):
        greet(dec=side_x)
        greet(dec=side_x, enc=above_z)
        greet(dec=side_x, enc=below_z)

    @pl.when(x > 0)
    def _():
        greet_side(x - 1)

    @pl.when(x < dec - 1)
    def _():
        greet_side(x + 1)

    sides = (x + dec - 1) // dec + 1 - (x + 1) // dec
    pl.semaphore_wait(barrier, enc + (1 if split else 0) + 3 * sides)

    start_own(0, 0, 1)
    local[0].wait()
    rows = 32

    def wide(ref):
        return jnp.concatenate([ref[i : i + 1, :] for i in range(ref.shape[0])], axis=1)

    gains[0:1, :] = wide(gain_pre)
    gains[1:2, :] = wide(gain_post)

    def first_norm(i, carry):
        at = pl.ds(pl.multiple_of(i * rows, rows), rows)
        normed[at, :] = layer_norm(xs[at, :].astype(jnp.float32), gains[0:1, :]).astype(jnp.bfloat16)
        return carry

    norm_steps = total // rows
    lax.fori_loop(0, norm_steps // 2, first_norm, 0)
    z_step(0, 1)
    lax.fori_loop(norm_steps // 2, norm_steps, first_norm, 0)
    for far in range(2, enc - 1):
        z_step(0, far)
    start_own(0, 1, 2)
    start_own(1, 0, 1)

    side = TS
    slots = total // (side * side)
    part = slots // 2
    row_groups = side // enc
    run = row_groups * side
    band = denom.shape[0] // spread_rows
    places = spread_rows * band
    lanes = enc * part * run
    lane = lax.broadcasted_iota(jnp.int32, (1, lanes), 1)
    strip_row = lax.broadcasted_iota(jnp.int32, (spread_rows, band, lanes), 0) * enc + z
    strip_row = strip_row.reshape(places, lanes)
    band_col = lax.broadcasted_iota(jnp.int32, (spread_rows, band, lanes), 1).reshape(places, lanes)

    def spread_of(owner):
        top = jnp.zeros((1, lanes), jnp.int32)
        left = jnp.zeros((1, lanes), jnp.int32)
        group = jnp.zeros((1, lanes), jnp.int32)
        col = lane
        for unit in range(enc * part):
            entry = (unit // part) * slots + owner * part + unit % part
            inside = lane >= unit * run
            top = jnp.where(inside, table[0, 0, entry], top)
            left = jnp.where(inside, table[0, 1, entry], left)
            for g in range(row_groups):
                begin = lane >= unit * run + g * side
                group = jnp.where(begin, g, group)
                col = jnp.where(begin, lane - (unit * run + g * side), col)
        tile_row = jnp.bitwise_and(group * enc + z - top, side - 1)
        middle = (side - 1) / 2.0
        dr = tile_row.astype(jnp.float32) - middle
        dc = col.astype(jnp.float32) - middle
        weight = jnp.exp(-(dr * dr + dc * dc) / (2.0 * blend_sigma * blend_sigma))
        weight = weight.astype(jnp.bfloat16).astype(jnp.float32)
        weight = jnp.where(top >= 0, weight, 0.0)
        hit = (strip_row == top + tile_row) & (band_col == left + col)
        return jnp.where(hit, weight, 0.0)

    mine_spread = spread_of(m)
    spread[...] = mine_spread.astype(jnp.bfloat16)
    denom[...] = jnp.sum(mine_spread + spread_of(1 - m), axis=1, keepdims=True)

    far_all = range(1, enc)
    if enc > 2:
        z_step(0, enc - 1)
    for far in range(2, enc):
        plane_step(0, far)
    z_step(1, 1)
    plane_step(0, 1)
    for far in far_all:
        diagonal_step(0, far)
    local[1].wait()

    col_steps = ff // COLS
    units = col_steps * 2

    def up_unit(i, carry):
        at = pl.ds(pl.multiple_of((i % 2) * half, half), half)
        cols = pl.ds(pl.multiple_of((i // 2) * COLS, COLS), COLS)
        value = jnp.dot(normed[at, :], weights[0, :, cols], preferred_element_type=jnp.float32)
        value = 0.5 * value * (1.0 + lax.erf(value * 0.7071067811865476))
        hidden[at, cols] = value.astype(jnp.bfloat16)
        return carry

    edges = [0, units // 5, units // 2, units * 7 // 10, units]
    lax.fori_loop(edges[0], edges[1], up_unit, 0)
    for far in range(2, enc - 1):
        z_step(1, far)
    start_own(1, 1, 2)
    lax.fori_loop(edges[1], edges[2], up_unit, 0)
    if enc > 2:
        z_step(1, enc - 1)
    for far in range(2, enc - 1):
        plane_step(1, far)
    lax.fori_loop(edges[2], edges[3], up_unit, 0)
    if enc > 2:
        plane_step(1, enc - 1)
    lax.fori_loop(edges[3], edges[4], up_unit, 0)
    plane_step(1, 1)
    for far in far_all:
        diagonal_step(1, far)
    local[2].wait()

    def exchange(i):
        cols = pl.ds(pl.multiple_of(i * COLS, COLS), COLS)
        return pltpu.make_async_remote_copy(
            src_ref=give.at[1 - m, :, cols], dst_ref=take.at[:, cols],
            send_sem=give_sem.at[i], recv_sem=take_sem.at[i],
            device_id={"mp": 1 - m}, device_id_type=MESH,
        )

    def down(i, carry):
        cols = pl.ds(pl.multiple_of(i * COLS, COLS), COLS)
        value = lax.dot_general(
            hidden[...], weights[1, cols, :], (((1,), (1,)), ((), ())),
            preferred_element_type=jnp.float32,
        ).astype(jnp.bfloat16)
        give[0, :, cols] = value[:half]
        give[1, :, cols] = value[half:]
        exchange(i).start()
        return carry

    steps = width // COLS
    lax.fori_loop(0, steps, down, 0)
    for i in range(steps):
        exchange(i).wait_recv()

    def second_norm(i, carry):
        at = pl.ds(pl.multiple_of(i * rows, rows), rows)
        whole = pl.ds(pl.multiple_of(m * half + i * rows, rows), rows)
        mixed = give[m, at, :].astype(jnp.float32) + take[at, :].astype(jnp.float32)
        value = xs[whole, :].astype(jnp.float32) + mixed
        normed[at, :] = layer_norm(value, gains[1:2, :]).astype(jnp.bfloat16)
        return carry

    lax.fori_loop(0, half // rows, second_norm, 0)
    local[3].wait()
    values = jnp.dot(
        normed[0:half, :], neck[...], preferred_element_type=jnp.float32
    ).astype(jnp.bfloat16)
    tile_size = side * side
    for slot in range(part):
        value = values[slot * tile_size : (slot + 1) * tile_size]
        top = table[0, 0, z * slots + m * part + slot]
        swapped = jnp.concatenate([value[tile_size // 2 :], value[: tile_size // 2]], axis=0)
        flag = jnp.bitwise_and(jnp.maximum(top, 0), side - 1) == side // 2
        value = jnp.where(flag, swapped.astype(jnp.float32), value.astype(jnp.float32)).astype(jnp.bfloat16)
        for row in range(side):
            at = slot * run + (row // enc) * side
            deal[row % enc, at : at + side, :] = value[row * side : (row + 1) * side]

    def deal_copy(off):
        target = (z + off) % enc
        return pltpu.make_async_remote_copy(
            src_ref=deal.at[target], dst_ref=dealt.at[z],
            send_sem=deal_send.at[off], recv_sem=deal_recv.at[off],
            device_id={"enc": target}, device_id_type=MESH,
        )

    for off in range(1, enc):
        deal_copy(off).start()
    dealt[z] = deal[z]
    local[4].wait()
    for off in range(1, enc):
        deal_copy(off).wait_recv()
    channels = deal.shape[2]
    numer = jnp.dot(
        spread[...], dealt[...].reshape(lanes, channels), preferred_element_type=jnp.float32
    )
    part_sum[...] = numer.astype(jnp.bfloat16)

    def pair(src, dst, which):
        return pltpu.make_async_remote_copy(
            src_ref=src, dst_ref=dst, send_sem=pair_send.at[which], recv_sem=pair_recv.at[which],
            device_id={"mp": 1 - m}, device_id_type=MESH,
        )

    swap_sum = pair(part_sum, other_sum, 0)
    swap_sum.start()
    swap_sum.wait_recv()
    numer = part_sum[...].astype(jnp.float32) + other_sum[...].astype(jnp.float32)
    whole = numer / denom[...]
    merged[...] = whole.astype(jnp.bfloat16)

    def halo_copy(which):
        return pltpu.make_async_remote_copy(
            src_ref=merged, dst_ref=halo.at[which],
            send_sem=halo_send.at[which], recv_sem=halo_recv.at[which],
            device_id={"enc": (below_z, above_z)[which]}, device_id_type=MESH,
        )

    halo_copy(0).start()
    halo_copy(1).start()
    cube = whole.reshape(spread_rows, band, channels)
    blank = jnp.zeros((edge.shape[1] - spread_rows, channels), jnp.float32)
    edge[0] = jnp.concatenate([cube[:, 0, :], blank], axis=0).astype(jnp.bfloat16)
    edge[1] = jnp.concatenate([cube[:, band - 1, :], blank], axis=0).astype(jnp.bfloat16)

    def edge_copy(which, level):
        target = {"dec": (x - 1, x + 1)[which]}
        if level:
            target["enc"] = (below_z, above_z)[level - 1]
        return pltpu.make_async_remote_copy(
            src_ref=edge.at[which], dst_ref=edges_in.at[1 - which, level],
            send_sem=edge_send.at[which, level], recv_sem=edge_recv.at[1 - which, level],
            device_id=target, device_id_type=MESH,
        )

    def every_edge(which, act):
        @pl.when((x > 0) if which == 0 else (x < dec - 1))
        def _():
            for level in range(3):
                act(edge_copy(which, level))

    every_edge(0, lambda c: c.start())
    every_edge(1, lambda c: c.start())

    kinds = conv_w.shape[3]

    def products(source, row_off):
        return [
            jnp.dot(source, conv_w[row_off, b], preferred_element_type=jnp.float32) for b in range(3)
        ]

    spot = lax.broadcasted_iota(jnp.int32, (spread_rows, band, kinds), 0).reshape(places, kinds)
    spot_col = lax.broadcasted_iota(jnp.int32, (spread_rows, band, kinds), 1).reshape(places, kinds)
    center = products(merged[...], 1)

    def moved_down(value, step, index):
        shifted_value = jnp.where(index == 0, 0.0, pltpu.roll(value, step, 0))
        return jnp.where(z == 0, shifted_value, value)

    def moved_up(value, step, index):
        size = value.shape[0]
        shifted_value = jnp.where(index == spread_rows - 1, 0.0, pltpu.roll(value, size - step, 0))
        return jnp.where(z == enc - 1, shifted_value, value)

    halo_copy(0).wait_recv()
    upper = products(halo[0], 0)
    halo_copy(1).wait_recv()
    lower = products(halo[1], 2)
    for which in range(2):
        every_edge(1 - which, lambda c: c.wait_send())

    @pl.when(x < dec - 1)
    def _():
        for level in range(3):
            edge_copy(0, level).wait_recv()

    @pl.when(x > 0)
    def _():
        for level in range(3):
            edge_copy(1, level).wait_recv()

    sums = [
        center[b] + moved_down(upper[b], band, spot) + moved_up(lower[b], band, spot) for b in range(3)
    ]
    index = lax.broadcasted_iota(jnp.int32, (edge.shape[1], kinds), 0)

    def edge_sum(which, b):
        levels = [
            jnp.dot(edges_in[which, level], conv_w[a, b], preferred_element_type=jnp.float32)
            for level, a in ((0, 1), (1, 0), (2, 2))
        ]
        value = levels[0] + moved_down(levels[1], 1, index) + moved_up(levels[2], 1, index)
        value = value[:spread_rows].reshape(spread_rows, 1, kinds)
        return jnp.broadcast_to(value, (spread_rows, band, kinds)).reshape(places, kinds)

    before = jnp.where(spot_col == 0, edge_sum(0, 0), pltpu.roll(sums[0], 1, 0))
    after = jnp.where(spot_col == band - 1, edge_sum(1, 2), pltpu.roll(sums[2], places - 1, 0))
    activ = jnp.maximum(sums[1] + before + after + conv_bias[...], 0.0).astype(jnp.bfloat16)
    part_logits[...] = lax.dot_general(
        cls_t[...], activ, (((1,), (1,)), ((), ())), preferred_element_type=jnp.float32
    )
    swap_logits = pair(part_logits, other_logits, 1)
    swap_logits.start()
    swap_logits.wait_recv()
    classes = out.shape[1]
    square = (classes, classes)
    same = lax.broadcasted_iota(jnp.int32, square, 0) == lax.broadcasted_iota(jnp.int32, square, 1)
    bias = jnp.sum(jnp.where(same, cls_bias[...], 0.0), axis=1, keepdims=True)
    logits = part_logits[...] + other_logits[...] + bias
    wanted = jnp.concatenate([labels[k] for k in range(spread_rows)], axis=1)
    ids = lax.broadcasted_iota(jnp.int32, (classes, places), 0)
    picked = jnp.sum(jnp.where(ids == wanted, logits, 0.0), axis=0, keepdims=True)
    nll = jnp.log(jnp.sum(jnp.exp(logits), axis=0, keepdims=True)) - picked
    for k in range(spread_rows):
        out_nll[k] = nll[:, k * band : (k + 1) * band]
        out[k] = logits[:, k * band : (k + 1) * band].reshape(classes, 1, band)

    swap_sum.wait_send()
    swap_logits.wait_send()
    halo_copy(0).wait_send()
    halo_copy(1).wait_send()
    for off in range(1, enc):
        deal_copy(off).wait_send()
    finish_sends(0)
    finish_sends(1)
    for i in range(steps):
        exchange(i).wait_send()


def body(
    tokens,
    gain_pre,
    w_up,
    w_down,
    gain_post,
    w_neck,
    conv_weight,
    conv_bias,
    cls_weight,
    cls_bias,
    tile_table,
    labels,
):
    sizes = tuple(lax.axis_size(name) for name in ("groups", "enc", "dec"))
    enc = sizes[1]
    blk, ff = w_up.shape
    width = tokens.shape[-1]
    flat = tokens.reshape(-1, width)
    total = flat.shape[0]
    half = total // 2
    rows_local, _, band = labels.shape
    places = rows_local * band
    channels = w_neck.shape[1]
    classes = cls_weight.shape[1]
    dealt_rows = half // enc
    edge_rows = -(-rows_local // 16) * 16
    bf16, f32 = jnp.bfloat16, jnp.float32
    vmem = pl.BlockSpec(memory_space=pltpu.VMEM)
    anywhere = pl.BlockSpec(memory_space=pl.ANY)
    dma = pltpu.SemaphoreType.DMA
    logits, nll = pl.pallas_call(
        functools.partial(strip_kernel, sizes, rows_local),
        out_shape=(
            jax.ShapeDtypeStruct((rows_local, classes, 1, band), f32),
            jax.ShapeDtypeStruct(labels.shape, f32),
        ),
        in_specs=[anywhere, vmem, anywhere, anywhere, vmem, anywhere, anywhere, vmem, vmem,
                  pl.BlockSpec(memory_space=pltpu.SMEM), vmem, vmem],
        out_specs=(vmem, vmem),
        scratch_shapes=[
            pltpu.VMEM((2, width), f32),
            pltpu.VMEM((2, width, ff), bf16),
            pltpu.VMEM((total, width), bf16),
            pltpu.VMEM((total, width), bf16),
            pltpu.VMEM((total, ff), bf16),
            pltpu.VMEM((2, half, width), bf16),
            pltpu.VMEM((half, width), bf16),
            pltpu.VMEM(w_neck.shape, bf16),
            pltpu.VMEM(conv_weight.shape, bf16),
            pltpu.VMEM((enc, dealt_rows, channels), bf16),
            pltpu.VMEM((enc, dealt_rows, channels), bf16),
            pltpu.VMEM((places, half), bf16),
            pltpu.VMEM((places, 1), f32),
            pltpu.VMEM((places, channels), bf16),
            pltpu.VMEM((places, channels), bf16),
            pltpu.VMEM((places, channels), bf16),
            pltpu.VMEM((2, places, channels), bf16),
            pltpu.VMEM((2, edge_rows, channels), bf16),
            pltpu.VMEM((2, 3, edge_rows, channels), bf16),
            pltpu.VMEM((classes, places), f32),
            pltpu.VMEM((classes, places), f32),
            dma((5,)),
            dma((2, enc, 4)),
            dma((2, enc, 6)),
            dma((width // COLS,)),
            dma((width // COLS,)),
            dma((enc,)),
            dma((enc,)),
            dma((2,)),
            dma((2,)),
            dma((2,)),
            dma((2,)),
            dma((2, 3)),
            dma((2, 3)),
        ],
        compiler_params=pltpu.CompilerParams(
            collective_id=0, has_side_effects=True, vmem_limit_bytes=60 * 1024 * 1024
        ),
    )(
        flat, gain_pre.reshape(-1, 128), w_up, w_down.T, gain_post.reshape(-1, 128), w_neck,
        conv_weight, conv_bias.reshape(1, -1), cls_weight.T, jnp.swapaxes(tile_table, 1, 2),
        cls_bias.reshape(1, -1), labels,
    )
    logits = jnp.transpose(logits, (0, 2, 3, 1))
    return (logits, nll)


def solution(mesh):
    in_specs = (
        P(("groups", "dec"), "enc", None, None, None),
        P(),
        P("enc", "mp"),
        P("mp", "enc"),
        P(),
        P(),
        P(None, None, None, "mp"),
        P("mp"),
        P("mp", None),
        P(),
        P(("groups", "dec"), None, None),
        P(None, "enc", ("groups", "dec")),
    )
    out_specs = (P(None, "enc", ("groups", "dec"), None), P(None, "enc", ("groups", "dec")))
    return jax.shard_map(body, mesh=mesh, in_specs=in_specs, out_specs=out_specs, check_vma=False)
```
